128 devices in a mesh: rep: 8 (over x, y_lo), shard: 16 (over y_hi, z, core).
Axes of the slice: x: 4, y: 4 (y_hi: 2, y_lo: 2; y = y_hi * 2 + y_lo), z: 4, core: 2. Of those that a mesh axis runs over, the one named last changes fastest.
Arguments:
- tokens: bfloat16 [2, 8192, 1536], P(None, ('rep', 'shard')), may hold values from -6 to 6
- query_weight: bfloat16 [1536, 1536], P('shard'), may hold values from -0.15625 to 0.15625
- key_weight: bfloat16 [1536, 768], P('shard'), may hold values from -0.15625 to 0.15625
- value_weight: bfloat16 [1536, 768], P('shard'), may hold values from -0.15625 to 0.15625
- out_weight: bfloat16 [1536, 1536], P('shard'), may hold values from -0.4375 to 0.4375
- gate_weight: bfloat16 [1536, 4096], P('shard'), may hold values from -0.15625 to 0.15625
- up_weight: bfloat16 [1536, 4096], P('shard'), may hold values from -0.15625 to 0.15625
- down_weight: bfloat16 [4096, 1536], P('shard'), may hold values from -0.09375 to 0.09375
- attention_gain: bfloat16 [1536], P('shard'), may hold values from 0.5 to 1.5
- feedforward_gain: bfloat16 [1536], P('shard'), may hold values from 0.5 to 1.5
- lengths: int32 [2, 8, 32], P(None, 'rep'), may hold values from 19 to 43, as said below
- deal: int32 [2, 8, 32], P(None, 'rep'), may hold values from 0 to 31, as said below
- block_cotangent: bfloat16 [2, 8192, 1536], P(None, ('rep', 'shard')), may hold values from -6 to 6
Outputs:
- block_out: bfloat16 [2, 8192, 1536], P(None, ('rep', 'shard'))
- input_grad: bfloat16 [2, 8192, 1536], P(None, ('rep', 'shard'))
- grad_query: float32 [1536, 1536], P('shard')
- grad_key: float32 [1536, 768], P('shard')
- grad_value: float32 [1536, 768], P('shard')
- grad_output: float32 [1536, 1536], P('shard')
- grad_gate: float32 [1536, 4096], P('shard')
- grad_up: float32 [1536, 4096], P('shard')
- grad_down: float32 [4096, 1536], P('shard')
- grad_attention_gain: float32 [1536], P('shard')
- grad_feedforward_gain: float32 [1536], P('shard')
The draws below stay inside these ranges and needn't reach their ends.
Inputs may be any that keep to these rules, and one draw needn't show every extreme that they name: `lengths`: for each micro-batch and replica group, the 2 sequences that deal places into one bin have between (585) // 10 and 64 tokens together, and some bin of the group has exactly 64. `deal`: for each micro-batch and replica group, a permutation of the group's 32 sequence numbers; entry b * 2 + s names the sequence in place s of bin b.
All inputs are finite; a program needn't handle non-finite values.
Results may differ from the reference program's by a relative error of at most 0.023.
Values may be sent and summed in bfloat16 or wider, within the bound.
A program may use at most 320 MiB of HBM per device.

```python
import math
import jax
import jax.numpy as jnp
from jax import lax

D = 1536
QUERY_HEADS = 16
KEY_VALUE_HEADS = 8
HEAD_WIDTH = 96
FF = 4096
BIN = 64
MB = 2
SEQ_BIN = 2
KVW = 768
GROUPS = 8
BINS = 16
NSEQ = 32
ROWS = 8192


def dealt_sequences(key):
    groups_all = MB * GROUPS
    order_keys = jax.random.split(jax.random.fold_in(key, 101), groups_all)
    orders = jax.vmap(lambda single: jax.random.permutation(single, NSEQ))(order_keys).astype(jnp.int32)
    floor_total = (9 * BIN + 9) // 10
    totals = jax.random.randint(jax.random.fold_in(key, 202), (groups_all, BINS), floor_total, BIN + 1).astype(jnp.int32)
    full_bin = jax.random.randint(jax.random.fold_in(key, 303), (groups_all, 1), 0, BINS).astype(jnp.int32)
    least_bin = ((full_bin + 1) % BINS).astype(jnp.int32)
    bin_ids = jnp.arange(BINS, dtype=jnp.int32)[None, :]
    totals = jnp.where(bin_ids == full_bin, BIN, totals).astype(jnp.int32)
    totals = jnp.where(bin_ids == least_bin, floor_total, totals).astype(jnp.int32)
    shares = jax.random.randint(jax.random.fold_in(key, 404), (groups_all, BINS, SEQ_BIN), 2, 5).astype(jnp.int32)
    fixed_shares = jnp.where(jnp.arange(SEQ_BIN, dtype=jnp.int32) == SEQ_BIN - 1, 4, 2).astype(jnp.int32)[None, None, :]
    pinned = ((bin_ids == full_bin) | (bin_ids == least_bin))[:, :, None]
    shares = jnp.where(pinned, fixed_shares, shares).astype(jnp.int32)
    share_sum = jnp.sum(shares, axis=2, keepdims=True).astype(jnp.int32)
    pieces = (totals[:, :, None] * shares // share_sum).astype(jnp.int32)
    leftover = (totals - jnp.sum(pieces, axis=2)).astype(jnp.int32)
    last_place = jnp.arange(SEQ_BIN, dtype=jnp.int32)[None, None, :] == SEQ_BIN - 1
    pieces = jnp.where(last_place, pieces + leftover[:, :, None], pieces).astype(jnp.int32)
    slot_lengths = pieces.reshape(groups_all, NSEQ)
    seq_lengths = jax.vmap(lambda order, slot: jnp.zeros((NSEQ,), jnp.int32).at[order].set(slot))(orders, slot_lengths)
    return (orders.reshape(MB, GROUPS, NSEQ), seq_lengths.reshape(MB, GROUPS, NSEQ).astype(jnp.int32))


def draw_lengths(key, part):
    return dealt_sequences(key)[1]


def draw_deal(key, part):
    return dealt_sequences(key)[0]


def shard_levels(own_key, extent, shards, low, high):
    loudness, own = 1.0, jax.random.fold_in(own_key, 6)
    for axis_at, shards_of in shards:
        heights = jnp.exp(jax.random.uniform(jax.random.fold_in(own, axis_at), (shards_of,), jnp.float32, low / len(shards), high / len(shards)))
        loudness = loudness * jnp.repeat(heights, extent[axis_at] // shards_of).reshape([-1 if axis == axis_at else 1 for axis in range(len(extent))])
    return loudness


def scatter_about(stream_key, extent, width, most, cuts=(), kind=jnp.bfloat16):
    values = width * jax.random.normal(stream_key, extent, jnp.float32)
    if cuts:
        values = values * shard_levels(stream_key, extent, cuts, -0.22, 0.18)
    return jnp.clip(values, -most, most).astype(kind)


def setup_inputs(seed: int = 0) -> dict:
    splits = jax.random.split(jax.random.key(seed), 14)
    tokens = scatter_about(splits[0], (MB, ROWS, D), 1.0, 6.0, ((1, 128),))
    query_weight = scatter_about(splits[1], (D, D), D ** -0.5, 0.15625, ((0, 16),))
    key_weight = scatter_about(splits[2], (D, KVW), D ** -0.5, 0.15625, ((0, 16),))
    value_weight = scatter_about(splits[3], (D, KVW), D ** -0.5, 0.15625, ((0, 16),))
    out_weight = scatter_about(splits[4], (D, D), (D // 8) ** -0.5, 0.4375, ((0, 16),))
    gate_weight = scatter_about(splits[5], (D, FF), D ** -0.5, 0.15625, ((0, 16),))
    up_weight = scatter_about(splits[6], (D, FF), D ** -0.5, 0.15625, ((0, 16),))
    down_weight = scatter_about(splits[7], (FF, D), FF ** -0.5, 0.09375, ((0, 16),))
    attention_gain = jnp.clip(1.0 + 0.1 * jax.random.normal(splits[8], (D,), jnp.float32), 0.5, 1.5).astype(jnp.bfloat16)
    feedforward_gain = jnp.clip(1.0 + 0.1 * jax.random.normal(splits[9], (D,), jnp.float32), 0.5, 1.5).astype(jnp.bfloat16)
    lengths = draw_lengths(jax.random.fold_in(splits[13], 71), 0)
    deal = draw_deal(jax.random.fold_in(splits[13], 71), 0)
    block_cotangent = scatter_about(splits[12], (MB, ROWS, D), 1.0, 6.0, ((1, 128),))
    return {"tokens": tokens, "query_weight": query_weight, "key_weight": key_weight, "value_weight": value_weight, "out_weight": out_weight, "gate_weight": gate_weight, "up_weight": up_weight, "down_weight": down_weight, "attention_gain": attention_gain, "feedforward_gain": feedforward_gain, "lengths": lengths, "deal": deal, "block_cotangent": block_cotangent}


eps_norm = 1e-05
rope_base = 100000.0
highest = lax.Precision.HIGHEST

@jax.custom_vjp
def lower_precision(v):
    return lax.optimization_barrier(v.astype(jnp.bfloat16)).astype(jnp.float32)

@jax.custom_vjp
def low_back(v):
    return v

def low_keep(v):
    return (lower_precision(v), None)

def low_pass(kept, grad):
    return (grad,)

def back_keep(v):
    return (v, None)

def back_low(kept, grad):
    return (lower_precision(grad),)
lower_precision.defvjp(low_keep, low_pass)
low_back.defvjp(back_keep, back_low)

def sequence_tables(seq_lengths, seq_deal):
    count = seq_lengths.shape[0]
    seq_ids = jnp.arange(count, dtype=jnp.int32)
    seq_start = (jnp.cumsum(seq_lengths) - seq_lengths).astype(jnp.int32)
    matched = seq_deal[:, None] == seq_ids[None, :]
    slot_length = lax.optimization_barrier(jnp.sum(jnp.where(matched, seq_lengths[None, :], 0), axis=1)).astype(jnp.int32)
    slot_source = lax.optimization_barrier(jnp.sum(jnp.where(matched, seq_start[None, :], 0), axis=1)).astype(jnp.int32)
    slot_of_seq = lax.optimization_barrier(jnp.sum(jnp.where(matched, seq_ids[:, None], 0), axis=0)).astype(jnp.int32)
    per_bin = slot_length.reshape(-1, SEQ_BIN)
    slot_begin = (jnp.cumsum(per_bin, axis=1) - per_bin).reshape(-1).astype(jnp.int32)
    return (seq_start, slot_length, slot_source, slot_of_seq, slot_begin)

def bin_layout(tables, bin_index, token_rows):
    seq_start, slot_length, slot_source, slot_of_seq, slot_begin = tables
    first = (bin_index * SEQ_BIN).astype(jnp.int32)
    lengths_here = lax.dynamic_slice_in_dim(slot_length, first, SEQ_BIN)
    begins_here = lax.dynamic_slice_in_dim(slot_begin, first, SEQ_BIN)
    sources_here = lax.dynamic_slice_in_dim(slot_source, first, SEQ_BIN)
    row_ids = jnp.arange(token_rows, dtype=jnp.int32)
    ends_here = begins_here + lengths_here
    segment = lax.optimization_barrier(jnp.sum((row_ids[:, None] >= ends_here[None, :]).astype(jnp.int32), axis=1)).astype(jnp.int32)
    onehot = segment[:, None] == jnp.arange(SEQ_BIN, dtype=jnp.int32)[None, :]
    token_position = (row_ids - lax.optimization_barrier(jnp.sum(jnp.where(onehot, begins_here[None, :], 0), axis=1))).astype(jnp.int32)
    source = (lax.optimization_barrier(jnp.sum(jnp.where(onehot, sources_here[None, :], 0), axis=1)) + token_position).astype(jnp.int32)
    return (source, segment < SEQ_BIN, segment, token_position)

def order_layout(tables, seq_lengths, row_ids, token_rows):
    seq_start, slot_length, slot_source, slot_of_seq, slot_begin = tables
    count = seq_lengths.shape[0]
    seq_end = seq_start + seq_lengths
    which = lax.optimization_barrier(jnp.sum((row_ids[:, None] >= seq_end[None, :]).astype(jnp.int32), axis=1)).astype(jnp.int32)
    onehot = which[:, None] == jnp.arange(count, dtype=jnp.int32)[None, :]
    inner = (row_ids - lax.optimization_barrier(jnp.sum(jnp.where(onehot, seq_start[None, :], 0), axis=1))).astype(jnp.int32)
    slot = lax.optimization_barrier(jnp.sum(jnp.where(onehot, slot_of_seq[None, :], 0), axis=1)).astype(jnp.int32)
    slot_hot = slot[:, None] == jnp.arange(count, dtype=jnp.int32)[None, :]
    begin = lax.optimization_barrier(jnp.sum(jnp.where(slot_hot, slot_begin[None, :], 0), axis=1)).astype(jnp.int32)
    target = (slot // SEQ_BIN * token_rows + begin + inner).astype(jnp.int32)
    return (target, which < count)

def rotary_apply(value_rows, token_position):
    half = value_rows.shape[-1] // 2
    freq = jnp.exp(jnp.arange(half, dtype=jnp.float32) * (-2.0 * math.log(rope_base) / value_rows.shape[-1]))
    angle = token_position.astype(jnp.float32)[:, None] * freq[None, :]
    cosine_table = jnp.cos(angle)[:, None, :]
    sine_table = jnp.sin(angle)[:, None, :]
    first = value_rows[..., :half]
    second = value_rows[..., half:]
    return jnp.concatenate([first * cosine_table - second * sine_table, second * cosine_table + first * sine_table], axis=-1)

def block(rows_in, segment, token_position, params):
    query_weight, key_weight, value_weight, out_weight, gate_weight, up_weight, down_weight, attention_gain, feedforward_gain = params
    token_rows = rows_in.shape[0]
    inverse1 = lax.rsqrt(lax.optimization_barrier(jnp.mean(rows_in * rows_in, axis=-1, keepdims=True)) + eps_norm)
    normed1 = lower_precision(rows_in * inverse1 * attention_gain)
    query_projection = low_back(jnp.dot(normed1, query_weight, precision=highest))
    key_projection = low_back(jnp.dot(normed1, key_weight, precision=highest))
    value_projection = low_back(jnp.dot(normed1, value_weight, precision=highest))
    query_rows = lower_precision(rotary_apply(query_projection.reshape(token_rows, QUERY_HEADS, HEAD_WIDTH), token_position)).reshape(token_rows, KEY_VALUE_HEADS, QUERY_HEADS // KEY_VALUE_HEADS, HEAD_WIDTH)
    rotated_keys = lower_precision(rotary_apply(key_projection.reshape(token_rows, KEY_VALUE_HEADS, HEAD_WIDTH), token_position))
    value_rows = lower_precision(value_projection).reshape(token_rows, KEY_VALUE_HEADS, HEAD_WIDTH)
    raw = jnp.einsum('ihgd,jhd->hgij', query_rows, rotated_keys, precision=highest)
    scores = low_back(raw * HEAD_WIDTH ** (-0.5))
    row_ids = jnp.arange(token_rows, dtype=jnp.int32)
    allowed = (segment[:, None] == segment[None, :]) & (row_ids[None, :] <= row_ids[:, None])
    scores = jnp.where(allowed, scores, -1e+30)
    probs = jax.nn.softmax(scores, axis=-1)
    mixed = jnp.einsum('hgij,jhd->ihgd', lower_precision(probs), value_rows, precision=highest).reshape(token_rows, QUERY_HEADS * HEAD_WIDTH)
    mixed = low_back(lower_precision(mixed))
    resid = rows_in + low_back(jnp.dot(mixed, out_weight, precision=highest))
    inverse2 = lax.rsqrt(lax.optimization_barrier(jnp.mean(resid * resid, axis=-1, keepdims=True)) + eps_norm)
    normed2 = lower_precision(resid * inverse2 * feedforward_gain)
    gate = low_back(jnp.dot(normed2, gate_weight, precision=highest))
    upper = low_back(jnp.dot(normed2, up_weight, precision=highest))
    hidden = lower_precision(jax.nn.silu(gate) * upper)
    return resid + low_back(jnp.dot(hidden, down_weight, precision=highest))

def reference(tokens, query_weight, key_weight, value_weight, out_weight, gate_weight, up_weight, down_weight, attention_gain, feedforward_gain, lengths, deal, block_cotangent):
    tables = jax.vmap(jax.vmap(sequence_tables))(lengths, deal)

    def group_bins(table):
        return jax.vmap(lambda index: bin_layout(table, index, BIN))(jnp.arange(BINS, dtype=jnp.int32))
    source, bin_valid, segment, token_position = jax.vmap(jax.vmap(group_bins))(tables)

    def group_order(table, seq_lengths):
        return order_layout(table, seq_lengths, jnp.arange(BINS * BIN, dtype=jnp.int32), BIN)
    target, order_valid = jax.vmap(jax.vmap(group_order))(tables, lengths)
    step = jax.checkpoint(lambda item, weights: block(item[0], item[1], item[2], weights))

    def forward(flat_in, params):
        grouped = flat_in.reshape(MB, GROUPS, BINS * BIN, D)
        picked = jax.vmap(jax.vmap(lambda rows_all, index: rows_all[index]))(grouped, source.reshape(MB, GROUPS, BINS * BIN))
        picked = jnp.where(bin_valid.reshape(MB, GROUPS, BINS * BIN)[..., None], picked, 0.0)
        bins_in = picked.reshape(-1, BIN, D)
        bins_out = lax.map(lambda item: step(item, params), (bins_in, segment.reshape(-1, BIN), token_position.reshape(-1, BIN)))
        grouped_out = bins_out.reshape(MB, GROUPS, BINS * BIN, D)
        back = jax.vmap(jax.vmap(lambda rows_all, index: rows_all[index]))(grouped_out, target)
        back = jnp.where(order_valid[..., None], back, 0.0)
        return back.reshape(MB, ROWS, D)
    params = tuple((weight.astype(jnp.float32) for weight in (query_weight, key_weight, value_weight, out_weight, gate_weight, up_weight, down_weight, attention_gain, feedforward_gain)))
    primal, pull = jax.vjp(forward, tokens.astype(jnp.float32), params)
    grad_in, grads = pull(block_cotangent.astype(jnp.float32))
    return (primal.astype(jnp.bfloat16), grad_in.astype(jnp.bfloat16), grads[0], grads[1], grads[2], grads[3], grads[4], grads[5], grads[6], grads[7], grads[8])
```

```python
import math

import jax
import jax.numpy as jnp
from jax import lax
from jax.sharding import PartitionSpec as P

D = 1536
QUERY_HEADS = 16
KEY_VALUE_HEADS = 8
HEAD_WIDTH = 96
QW = QUERY_HEADS * HEAD_WIDTH
KVW = KEY_VALUE_HEADS * HEAD_WIDTH
FF = 4096
BIN = 64
HALO = 48
WIN = BIN + HALO
MB = 2
SHARDS = 16

eps_norm = 1e-05
rope_base = 100000.0


def window_layout(seq_lengths, first_row):
    count = seq_lengths.shape[0]
    ids = jnp.arange(count, dtype=jnp.int32)
    earlier = ids[None, :] < ids[:, None]
    start = jnp.sum(jnp.where(earlier, seq_lengths[None, :], 0), axis=1)
    end = start + seq_lengths
    rows = first_row + jnp.arange(WIN, dtype=jnp.int32)
    which = jnp.sum((rows[:, None] >= end[None, :]).astype(jnp.int32), axis=1)
    onehot = which[:, None] == ids[None, :]
    begin = jnp.sum(jnp.where(onehot, start[None, :], 0), axis=1)
    inside = which < count
    mine = inside & (begin >= first_row) & (begin < first_row + BIN)
    return which, rows - begin, mine, inside


def rope_tables(position):
    half = HEAD_WIDTH // 2
    freq = jnp.exp(jnp.arange(half, dtype=jnp.float32) * (-2.0 * math.log(rope_base) / HEAD_WIDTH))
    angle = position.astype(jnp.float32)[:, None] * freq[None, :]
    return jnp.cos(angle)[:, None, :], jnp.sin(angle)[:, None, :]


def rotate(value, cos, sin):
    half = value.shape[-1] // 2
    first, second = value[..., :half], value[..., half:]
    return jnp.concatenate([first * cos - second * sin, second * cos + first * sin], axis=-1)


def dot(a, b, dims):
    return lax.dot_general(a, b, (dims, ((), ())), preferred_element_type=jnp.float32)


def nn(a, b):
    return dot(a, b, ((1,), (0,)))


def nt(a, b):
    return dot(a, b, ((1,), (1,)))


def tn(a, b):
    return dot(a, b, ((0,), (0,)))


def attention_forward(q, k, v, allowed):
    scale = HEAD_WIDTH ** (-0.5)
    s = jnp.einsum("mihgd,mjhd->mhgij", q, k, preferred_element_type=jnp.float32) * scale
    s = jnp.where(allowed, s, -1e30)
    peak = jnp.max(s, axis=-1, keepdims=True)
    e = jnp.exp(s - peak)
    p = e / jnp.sum(e, axis=-1, keepdims=True)
    p_low = p.astype(jnp.bfloat16)
    o = jnp.einsum("mhgij,mjhd->mihgd", p_low, v, preferred_element_type=jnp.float32)
    return p, p_low, o.astype(jnp.bfloat16)


def layer_pass(x_low, dy, which, position, layer):
    wq, wk, wv, wo, wg, wu, wd, gain1, gain2 = layer
    rows = x_low.shape[0]
    group = QUERY_HEADS // KEY_VALUE_HEADS
    scale = HEAD_WIDTH ** (-0.5)
    gain1 = gain1.astype(jnp.float32)
    gain2 = gain2.astype(jnp.float32)
    x = x_low.astype(jnp.float32)
    r1 = lax.rsqrt(jnp.mean(x * x, axis=-1, keepdims=True) + eps_norm)
    n1 = x * r1
    a1 = (n1 * gain1).astype(jnp.bfloat16)
    cos, sin = rope_tables(position)
    q = rotate(nn(a1, wq).reshape(rows, QUERY_HEADS, HEAD_WIDTH), cos, sin).astype(jnp.bfloat16)
    k = rotate(nn(a1, wk).reshape(rows, KEY_VALUE_HEADS, HEAD_WIDTH), cos, sin).astype(jnp.bfloat16)
    v = nn(a1, wv).astype(jnp.bfloat16)
    q = q.reshape(MB, WIN, KEY_VALUE_HEADS, group, HEAD_WIDTH)
    k = k.reshape(MB, WIN, KEY_VALUE_HEADS, HEAD_WIDTH)
    v = v.reshape(MB, WIN, KEY_VALUE_HEADS, HEAD_WIDTH)
    seg = which.reshape(MB, WIN)
    ids = jnp.arange(WIN, dtype=jnp.int32)
    allowed = (seg[:, :, None] == seg[:, None, :]) & (ids[None, :] <= ids[:, None])[None]
    allowed = allowed[:, None, None]
    p, p_low, o = attention_forward(q, k, v, allowed)
    o = o.reshape(rows, QW)
    x2 = x + nn(o, wo)
    r2 = lax.rsqrt(jnp.mean(x2 * x2, axis=-1, keepdims=True) + eps_norm)
    n2 = x2 * r2
    a2 = (n2 * gain2).astype(jnp.bfloat16)
    g = nn(a2, wg)
    u = nn(a2, wu)
    sig = jax.nn.sigmoid(g)
    sw = g * sig
    hid = (sw * u).astype(jnp.bfloat16)
    block_rows = (x2 + nn(hid, wd)).astype(jnp.bfloat16)

    dhid = nt(dy, wd)
    dg = (dhid * u * sig * (1.0 + g * (1.0 - sig))).astype(jnp.bfloat16)
    du = (dhid * sw).astype(jnp.bfloat16)
    gw_down = tn(hid, dy)
    gw_gate = tn(a2, dg)
    gw_up = tn(a2, du)
    da2 = nt(dg, wg) + nt(du, wu)
    g_gain2 = jnp.sum(da2 * n2, axis=0)
    e2 = da2 * gain2
    dx2 = dy.astype(jnp.float32) + r2 * (e2 - n2 * jnp.mean(e2 * n2, axis=-1, keepdims=True))
    dat = dx2.astype(jnp.bfloat16)
    gw_out = tn(o, dat)
    do = nt(dat, wo).astype(jnp.bfloat16).reshape(MB, WIN, KEY_VALUE_HEADS, group, HEAD_WIDTH)
    dp = jnp.einsum("mihgd,mjhd->mhgij", do, v, preferred_element_type=jnp.float32)
    spread = jnp.sum(p * dp, axis=-1, keepdims=True)
    ds = (p * (dp - spread)).astype(jnp.bfloat16)
    dq = jnp.einsum("mhgij,mjhd->mihgd", ds, k, preferred_element_type=jnp.float32) * scale
    dk = jnp.einsum("mhgij,mihgd->mjhd", ds, q, preferred_element_type=jnp.float32) * scale
    dv = jnp.einsum("mhgij,mihgd->mjhd", p_low, do, preferred_element_type=jnp.float32)
    dqf = rotate(dq.reshape(rows, QUERY_HEADS, HEAD_WIDTH), cos, -sin).reshape(rows, QW).astype(jnp.bfloat16)
    dkf = rotate(dk.reshape(rows, KEY_VALUE_HEADS, HEAD_WIDTH), cos, -sin).reshape(rows, KVW).astype(jnp.bfloat16)
    dvf = dv.reshape(rows, KVW).astype(jnp.bfloat16)
    gw_query = tn(a1, dqf)
    gw_key = tn(a1, dkf)
    gw_value = tn(a1, dvf)
    da1 = nt(dqf, wq) + nt(dkf, wk) + nt(dvf, wv)
    g_gain1 = jnp.sum(da1 * n1, axis=0)
    e1 = da1 * gain1
    dx = dx2 + r1 * (e1 - n1 * jnp.mean(e1 * n1, axis=-1, keepdims=True))
    grads = (gw_query, gw_key, gw_value, gw_out, gw_gate, gw_up, gw_down, g_gain1, g_gain2)
    return block_rows, dx.astype(jnp.bfloat16), grads


def body(
    tokens,
    query_weight,
    key_weight,
    value_weight,
    out_weight,
    gate_weight,
    up_weight,
    down_weight,
    attention_gain,
    feedforward_gain,
    lengths,
    deal,
    block_cotangent,
):
    me = lax.axis_index("shard")
    shards = (
        query_weight,
        key_weight,
        value_weight,
        out_weight,
        gate_weight,
        up_weight,
        down_weight,
        attention_gain,
        feedforward_gain,
    )
    both = jnp.stack([tokens, block_cotangent])
    ahead = [(d, d - 1) for d in range(1, SHARDS)]
    halo = lax.ppermute(both[:, :, :HALO], "shard", ahead)
    window = jnp.concatenate([both, halo], axis=2)
    layout = [window_layout(lengths[m, 0], me * BIN) for m in range(MB)]
    which = jnp.concatenate([one[0] for one in layout])
    position = jnp.concatenate([one[1] for one in layout])
    mine = jnp.concatenate([one[2] for one in layout])
    window = jnp.where(mine[None, :, None], window.reshape(2, MB * WIN, D), 0)
    layer = tuple(lax.all_gather(part, "shard", axis=0, tiled=True) for part in shards)
    position = jnp.where(mine, position, 0)
    block_rows, input_rows, grads = layer_pass(window[0], window[1], which, position, layer)
    results = jnp.stack([block_rows, input_rows]).reshape(2, MB, WIN, D)
    back = [(d, d + 1) for d in range(SHARDS - 1)]
    from_before = lax.ppermute(results[:, :, BIN:], "shard", back)
    from_before = jnp.pad(from_before, ((0, 0), (0, 0), (0, BIN - HALO), (0, 0)))
    mine_own = jnp.stack([one[2][:BIN] for one in layout])[None, :, :, None]
    inside = jnp.stack([one[3][:BIN] for one in layout])[None, :, :, None]
    rows_out = jnp.where(mine_own, results[:, :, :BIN], jnp.where(inside, from_before, 0))
    totals = []
    for part in grads:
        part = lax.psum_scatter(part.astype(jnp.bfloat16), "shard", scatter_dimension=0, tiled=True)
        totals.append(lax.psum(part, "rep").astype(jnp.float32))
    return (rows_out[0], rows_out[1], *totals)


def solution(mesh):
    placed = (
        P(None, ("rep", "shard"), None),
        *([P("shard", None)] * 7),
        P("shard"),
        P("shard"),
        P(None, "rep", None),
        P(None, "rep", None),
        P(None, ("rep", "shard"), None),
    )
    return jax.shard_map(
        body,
        mesh=mesh,
        in_specs=placed,
        out_specs=(
            P(None, ("rep", "shard"), None),
            P(None, ("rep", "shard"), None),
            *([P("shard", None)] * 7),
            P("shard"),
            P("shard"),
        ),
        check_vma=False,
    )
```

```python
import math

import jax
import jax.numpy as jnp
from jax import lax
from jax.experimental import pallas as pl
from jax.experimental.pallas import tpu as pltpu
from jax.sharding import PartitionSpec as P

D = 1536
QUERY_HEADS = 16
KEY_VALUE_HEADS = 8
HEAD_WIDTH = 96
QW = QUERY_HEADS * HEAD_WIDTH
KVW = KEY_VALUE_HEADS * HEAD_WIDTH
FF = 4096
BIN = 64
HALO = 48
WIN = BIN + HALO
MB = 2
SHARDS = 16
ROWS = MB * WIN
MESH = pl.DeviceIdType.MESH
ANY = pl.BlockSpec(memory_space=pl.ANY)
DMA = pltpu.SemaphoreType.DMA

eps_norm = 1e-05
rope_base = 100000.0


class Place:
    def __init__(self):
        rep, shard = lax.axis_index("rep"), lax.axis_index("shard")
        self.rep, self.shard = rep, shard
        self.x, self.yl = rep // 2, rep % 2
        self.yh, self.z, self.c = shard // 8, (shard // 2) % 4, shard % 2
        self.y = self.yh * 2 + self.yl
        self.half = jnp.where(self.yh == self.yl, 1, 0)

    def at(self, x=None, yh=None, yl=None, z=None, c=None):
        def pick(new, old):
            return old if new is None else new

        rep = pick(x, self.x) * 2 + pick(yl, self.yl)
        return rep, pick(yh, self.yh) * 8 + pick(z, self.z) * 2 + pick(c, self.c)

    def along(self, dim):
        found = []
        for o in (1, 2, 3):
            x, yh, yl, z = self.x, self.yh, self.yl, self.z
            if dim == "x":
                x = (x + o) % 4
            elif dim == "z":
                z = (z + o) % 4
            else:
                y = (self.y + o) % 4
                yh, yl = y // 2, y % 2
            found.append((x, yh, yl, z))
        return found

    def peers(self, dim):
        return [self.at(*where) for where in self.along(dim)]

    def cross(self):
        return self.at(yh=1 - self.yh, yl=1 - self.yl)

    def inner(self):
        return self.at(yl=1 - self.yl)

    def sibling(self):
        return self.at(c=1 - self.c)

    def step(self, by):
        return self.rep, (self.shard + by + SHARDS) % SHARDS


def meet(peers):
    barrier = pltpu.get_barrier_semaphore()
    for peer in peers:
        pl.semaphore_signal(barrier, inc=1, device_id=peer, device_id_type=MESH)
    pl.semaphore_wait(barrier, len(peers))


class Sender:
    def __init__(self):
        self.pending = []

    def __call__(self, src, dst, send_sem, recv_sem, to):
        copy = pltpu.make_async_remote_copy(
            src_ref=src,
            dst_ref=dst,
            send_sem=send_sem,
            recv_sem=recv_sem,
            device_id=to,
            device_id_type=MESH,
        )
        copy.start()
        self.pending.append(copy)
        return copy

    def drain(self):
        for copy in self.pending:
            copy.wait_send()


def cut(first, count):
    if isinstance(first, int):
        return pl.ds(first, count)
    return pl.ds(pl.multiple_of(first, 128), count)


def rcut(first, count):
    if isinstance(first, int):
        return pl.ds(first, count)
    return pl.ds(pl.multiple_of(first, 16), count)


GATE = 4
QUARTER = FF // 4
GATHER_UNITS = [(GATE, None, QUARTER), (7, 0, 256), (1, 0, 768), (2, 0, 768), (0, 0, 1536), (3, 0, 1536)]
GATHER_UNITS += [(5, i * 1024, 1024) for i in range(4)] + [(6, 0, 768), (6, 768, 768)]


def gather_kernel(*refs):
    ins, rows_in, outs, halo = refs[:8], refs[8:10], refs[10:18], refs[18]
    z_send, z_recv, y_send, y_recv, s_send, s_recv, x_send, x_recv, h_send, h_recv, local_sem = refs[19:]
    me = Place()
    meet(me.peers("z") + me.peers("x") + [me.cross(), me.inner(), me.sibling(), me.step(-1), me.step(1)])
    send = Sender()
    units = GATHER_UNITS
    local, z_sent, y_one, y_two, s_sent = {}, {}, {}, {}, []

    def columns(u, half=None):
        array, first, count = units[u]
        if first is None:
            first = me.x * QUARTER
        if half is None:
            return cut(first, count)
        return cut(first + half * (count // 2), count // 2)

    def z_phase(u):
        a = units[u][0]
        src, dst = ins[a].at[:, columns(u)], outs[a].at[me.yh, me.z, me.c, :, columns(u)]
        local[u] = pltpu.make_async_copy(src, dst, local_sem.at[u])
        local[u].start()
        z_sent[u] = [send(src, dst, z_send.at[u, i], z_recv.at[u, i], to) for i, to in enumerate(me.peers("z"))]

    def y_phase(u):
        a = units[u][0]
        local[u].wait()
        for copy in z_sent[u]:
            copy.wait_recv()
        ref = outs[a].at[me.yh, :, me.c, :, columns(u, me.half)]
        y_one[u] = send(ref, ref, y_send.at[u, 0], y_recv.at[u, 0], me.cross())
        if a != GATE:
            ref = outs[a].at[me.yh, :, me.c, :, columns(u)]
            s_sent.append(send(ref, ref, s_send.at[u, 0], s_recv.at[u, 0], me.sibling()))

    def forward_phase(u):
        a = units[u][0]
        y_one[u].wait_recv()
        ref = outs[a].at[1 - me.yh, :, me.c, :, columns(u, me.half)]
        y_two[u] = send(ref, ref, y_send.at[u, 1], y_recv.at[u, 1], me.inner())

    x_sent = []

    def last_phase(u):
        a = units[u][0]
        y_two[u].wait_recv()
        if a == GATE:
            ref = outs[a].at[:, :, me.c, :, columns(u)]
            for i, to in enumerate(me.peers("x")):
                x_sent.append(send(ref, ref, x_send.at[i], x_recv.at[i], to))
            s_sent.append(send(ref, ref, x_send.at[3], x_recv.at[3], me.sibling()))
        else:
            ref = outs[a].at[1 - me.yh, :, me.c, :, columns(u)]
            s_sent.append(send(ref, ref, s_send.at[u, 1], s_recv.at[u, 1], me.sibling()))

    for i, src in enumerate(rows_in):
        s_sent.append(send(src.at[:, pl.ds(0, HALO)], halo.at[i], h_send.at[i], h_recv.at[i], me.step(-1)))
    count = len(units)
    ahead = 2
    for u in range(ahead):
        z_phase(u)
    for t in range(count + 2):
        if t + ahead < count:
            z_phase(t + ahead)
        if t < count:
            y_phase(t)
        if 1 <= t <= count:
            forward_phase(t - 1)
        if t >= 2:
            last_phase(t - 2)
    for i in range(3):
        x_sent[i].wait_recv()
        quarter = (me.x + 3 - i) % 4
        ref = outs[GATE].at[:, :, me.c, :, cut(quarter * QUARTER, QUARTER)]
        s_sent.append(send(ref, ref, x_send.at[4 + i], x_recv.at[4 + i], me.sibling()))
    for copy in s_sent:
        copy.wait_recv()
    send.drain()


def gather_weights(parts, tokens, cotangent):
    count = len(GATHER_UNITS)
    outs = [jax.ShapeDtypeStruct((2, 4, 2, *part.shape), part.dtype) for part in parts]
    outs.append(jax.ShapeDtypeStruct((2, MB, HALO, D), jnp.bfloat16))
    results = pl.pallas_call(
        gather_kernel,
        out_shape=outs,
        in_specs=[ANY] * 10,
        out_specs=[ANY] * 9,
        scratch_shapes=[DMA((count, 3))] * 2 + [DMA((count, 2))] * 4 + [DMA((7,))] * 2 + [DMA((2,))] * 2 + [DMA((count,))],
        compiler_params=pltpu.CompilerParams(collective_id=1, has_side_effects=True),
        name="gather_weights",
    )(*parts, tokens, cotangent)
    return [full.reshape(-1, full.shape[-1]) for full in results[:8]], results[8]


def exchange_kernel(whole, *refs):
    count = len(whole)
    ins, outs = refs[:count], refs[count : 2 * count]
    send_sem, recv_sem, local_sem = refs[2 * count :]
    me = Place()
    meet([me.sibling()])
    send = Sender()
    copies = []
    for i, (src, dst) in enumerate(zip(ins, outs)):
        width = dst.shape[-1]
        theirs = src if whole[i] else src.at[:, cut((1 - me.c) * width, width)]
        own = src if whole[i] else src.at[:, cut(me.c * width, width)]
        copies.append(send(theirs, dst.at[me.c], send_sem.at[i], recv_sem.at[i], me.sibling()))
        local = pltpu.make_async_copy(own, dst.at[me.c], local_sem.at[i])
        local.start()
        copies.append(local)
    for copy in copies[1::2]:
        copy.wait()
    for copy in copies[::2]:
        copy.wait_recv()
    send.drain()


def exchange(arrays, whole):
    count = len(arrays)
    outs = []
    for array, full in zip(arrays, whole):
        rows, width = array.shape
        outs.append(jax.ShapeDtypeStruct((2, rows, width if full else width // 2), array.dtype))
    results = pl.pallas_call(
        lambda *refs: exchange_kernel(whole, *refs),
        out_shape=outs,
        in_specs=[ANY] * count,
        out_specs=[ANY] * count,
        scratch_shapes=[DMA((count,))] * 3,
        compiler_params=pltpu.CompilerParams(collective_id=2, has_side_effects=True),
        name="exchange_rows",
    )(*arrays)
    return [both.reshape(-1, both.shape[-1]) for both in results]


REDUCE_ROWS = (192, 192, 192, 192, 192, 512, 64)
REDUCE_COLUMNS = (768, 768, 768, 2048, 2048, 768, 256)
REDUCE_DIMS = {"A": "zyx", "B": "yxz", "C": "xzy"}
REDUCE_UNITS = [("A", 3, i * 512, 512) for i in range(4)] + [("A", 0, 0, 768)]
REDUCE_UNITS += [("B", 4, i * 512, 512) for i in range(4)] + [("B", 1, 0, 768)]
REDUCE_UNITS += [("C", 5, i * 256, 256) for i in range(3)] + [("C", 2, 0, 768), ("C", 6, 0, 256)]
ROUNDS = [(t, 5 + t, 10 + t) for t in range(5)]
GAINS = 6


def reduce_shapes(u):
    order, a, _, n = REDUCE_UNITS[u]
    r = REDUCE_ROWS[a]
    first = {"A": (2, r, n), "B": (4, r, n // 2), "C": (2, 4, r // 4, n)}[order]
    second = {"A": (r, n // 2), "B": (4, r // 4, n // 2), "C": (2, r // 4, n)}[order]
    return first, second, (r // 4, n // 2)


def add_into(total, parts):
    *lead, rows, _ = total.shape
    blocks = rows // 16

    def step(i, carry):
        where, rest = [], i // blocks
        for n in reversed(lead):
            where.insert(0, rest % n)
            rest = rest // n
        where = (*where, rcut((i % blocks) * 16, 16), slice(None))
        s = total[where].astype(jnp.float32)
        for k in range(3):
            s = s + parts[(k, *where)].astype(jnp.float32)
        total[where] = s.astype(jnp.bfloat16)
        return carry

    lax.fori_loop(0, math.prod(lead) * blocks, step, 0)


def reduce_kernel(*refs):
    nu = len(REDUCE_UNITS)
    ins, rows_in, outs, halo, totals = refs[:7], refs[7:9], refs[9:16], refs[16], refs[17:23]
    rest = refs[23:]
    kept = (rest[:nu], rest[nu : 2 * nu], rest[2 * nu : 3 * nu])
    taken = (rest[3 * nu : 4 * nu], rest[4 * nu : 5 * nu], rest[5 * nu : 6 * nu])
    send_sem, recv_sem, g_send, g_recv, s_send, s_recv, h_send, h_recv, local_sem, final_sem = rest[6 * nu :]
    totals = (*totals, outs[GAINS])
    me = Place()
    meet(me.peers("z") + me.peers("x") + me.peers("y") + [me.sibling(), me.step(-1), me.step(1)])
    send = Sender()
    sent, own = {}, {}

    def share(u, stage, x, yh, yl, z):
        order, a, first, n = REDUCE_UNITS[u]
        r = REDUCE_ROWS[a] // 4
        src = ins[a] if stage == 0 else kept[stage - 1][u]
        begin = first if stage == 0 else 0
        dim = REDUCE_DIMS[order][stage]
        lead = {"A": 2, "B": 2, "C": 2}[order] if stage == 0 else len(src.shape) - 2
        columns = slice(None) if stage else cut(begin, n)
        if dim == "z":
            return src.at[:, z, :, columns] if lead == 2 else src.at[z]
        if dim == "x":
            rows = rcut(x * r, r)
            if lead == 2:
                return src.at[:, :, rows, columns]
            return src.at[:, rows] if lead == 1 else src.at[rows]
        columns = cut(begin + yl * (n // 2), n // 2)
        if lead == 2:
            return src.at[yh, :, :, columns]
        return src.at[yh, :, columns]

    def issue(u, stage):
        dim = REDUCE_DIMS[REDUCE_UNITS[u][0]][stage]
        sent[u, stage] = [
            send(share(u, stage, *where), taken[stage][u].at[i], send_sem.at[u, stage, i], recv_sem.at[u, stage, i], me.at(*where))
            for i, where in enumerate(me.along(dim))
        ]
        own[u, stage] = pltpu.make_async_copy(
            share(u, stage, me.x, me.yh, me.yl, me.z), kept[stage][u], local_sem.at[u, stage]
        )
        own[u, stage].start()

    def finish(u, stage):
        own[u, stage].wait()
        for copy in sent[u, stage]:
            copy.wait_recv()
        add_into(kept[stage][u], taken[stage][u])

    def result(u, all_x, all_y):
        order, a, first, n = REDUCE_UNITS[u]
        r = REDUCE_ROWS[a] // 4
        rows = slice(None) if all_x else rcut(me.x * r, r)
        columns = cut(first, n) if all_y else cut(first + me.yl * (n // 2), n // 2)
        return totals[a].at[rows, columns]

    def spread_one(u):
        order = REDUCE_UNITS[u][0]
        dst = result(u, False, False)
        own[u, 3] = pltpu.make_async_copy(kept[2][u], dst, local_sem.at[u, 3])
        own[u, 3].start()
        to = [me.inner()] if order == "C" else me.peers("x")
        sent[u, 3] = [send(kept[2][u], dst, g_send.at[u, i], g_recv.at[u, i], one) for i, one in enumerate(to)]

    def spread_two(u):
        order = REDUCE_UNITS[u][0]
        own[u, 3].wait()
        for copy in sent[u, 3]:
            copy.wait_recv()
        ref = result(u, order != "C", order == "C")
        to = me.peers("x") if order == "C" else [me.inner()]
        sent[u, 4] = [send(ref, ref, g_send.at[u, 3 + i], g_recv.at[u, 3 + i], one) for i, one in enumerate(to)]

    last = []

    def deliver(u):
        order, a, first, n = REDUCE_UNITS[u]
        for copy in sent[u, 4]:
            copy.wait_recv()
        if a == GAINS:
            return
        r, width = REDUCE_ROWS[a] // 2, REDUCE_COLUMNS[a]
        dst = outs[a].at[:, cut(me.c * width + first, n)]
        last.append(send(totals[a].at[rcut((1 - me.c) * r, r), cut(first, n)], dst, s_send.at[u], s_recv.at[u], me.sibling()))
        own[u, 5] = pltpu.make_async_copy(totals[a].at[rcut(me.c * r, r), cut(first, n)], dst, final_sem.at[u])
        own[u, 5].start()

    for i, src in enumerate(rows_in):
        last.append(send(src.at[:, pl.ds(BIN, HALO)], halo.at[i], h_send.at[i], h_recv.at[i], me.step(1)))
    count = len(ROUNDS)
    for u in ROUNDS[0]:
        issue(u, 0)
    for t in range(count + 4):
        if t + 1 < count:
            for u in ROUNDS[t + 1]:
                issue(u, 0)
        for stage in range(2):
            if 0 <= t - stage < count:
                for u in ROUNDS[t - stage]:
                    finish(u, stage)
                    issue(u, stage + 1)
        if 0 <= t - 2 < count:
            for u in ROUNDS[t - 2]:
                finish(u, 2)
                spread_one(u)
        if 0 <= t - 3 < count:
            for u in ROUNDS[t - 3]:
                spread_two(u)
        if 0 <= t - 4 < count:
            for u in ROUNDS[t - 4]:
                deliver(u)
    for u in range(nu):
        if (u, 5) in own:
            own[u, 5].wait()
    for copy in last:
        copy.wait_recv()
    send.drain()


def reduce_grads(grads, block_rows, input_rows):
    nu = len(REDUCE_UNITS)
    first, second, third = zip(*[reduce_shapes(u) for u in range(nu)])
    low = jnp.bfloat16
    shapes = list(zip(REDUCE_ROWS, REDUCE_COLUMNS))
    outs = [jax.ShapeDtypeStruct((r // 2, 2 * n), low) for r, n in shapes[:GAINS]]
    outs.append(jax.ShapeDtypeStruct(shapes[GAINS], low))
    outs.append(jax.ShapeDtypeStruct((2, MB, HALO, D), low))
    outs += [jax.ShapeDtypeStruct(shape, low) for shape in shapes[:GAINS]]
    scratch = [pltpu.VMEM(s, low) for s in (*first, *second, *third)]
    scratch += [pltpu.VMEM((3, *s), low) for s in (*first, *second, *third)]
    scratch += [DMA((nu, 3, 3))] * 2 + [DMA((nu, 6))] * 2 + [DMA((nu,))] * 2 + [DMA((2,))] * 2 + [DMA((nu, 4)), DMA((nu,))]
    results = pl.pallas_call(
        reduce_kernel,
        out_shape=outs,
        in_specs=[ANY] * 9,
        out_specs=[ANY] * len(outs),
        scratch_shapes=scratch,
        compiler_params=pltpu.CompilerParams(collective_id=3, has_side_effects=True, vmem_limit_bytes=56 * 2**20),
        name="reduce_grads",
    )(*grads, block_rows, input_rows)
    return results[:GAINS], results[GAINS], results[GAINS + 1]


def window_layout(seq_lengths, first_row):
    count = seq_lengths.shape[0]
    ids = jnp.arange(count, dtype=jnp.int32)
    earlier = ids[None, :] < ids[:, None]
    start = jnp.sum(jnp.where(earlier, seq_lengths[None, :], 0), axis=1)
    end = start + seq_lengths
    rows = first_row + jnp.arange(WIN, dtype=jnp.int32)
    which = jnp.sum((rows[:, None] >= end[None, :]).astype(jnp.int32), axis=1)
    onehot = which[:, None] == ids[None, :]
    begin = jnp.sum(jnp.where(onehot, start[None, :], 0), axis=1)
    inside = which < count
    mine = inside & (begin >= first_row) & (begin < first_row + BIN)
    return which, rows - begin, mine, inside


def rope_tables(position):
    half = HEAD_WIDTH // 2
    freq = jnp.exp(jnp.arange(half, dtype=jnp.float32) * (-2.0 * math.log(rope_base) / HEAD_WIDTH))
    angle = position.astype(jnp.float32)[:, None] * freq[None, :]
    return jnp.cos(angle)[:, None, :], jnp.sin(angle)[:, None, :]


def rotate(value, cos, sin):
    half = value.shape[-1] // 2
    first, second = value[..., :half], value[..., half:]
    return jnp.concatenate([first * cos - second * sin, second * cos + first * sin], axis=-1)


def dot(a, b, dims):
    return lax.dot_general(a, b, (dims, ((), ())), preferred_element_type=jnp.float32)


def nn(a, b):
    return dot(a, b, ((1,), (0,)))


def nt(a, b):
    return dot(a, b, ((1,), (1,)))


def tn(a, b):
    return dot(a, b, ((0,), (0,)))


def attention_forward(q, k, v, allowed):
    scale = HEAD_WIDTH ** (-0.5)
    s = jnp.einsum("mihgd,mjhd->mhgij", q, k, preferred_element_type=jnp.float32) * scale
    s = jnp.where(allowed, s, -1e30)
    peak = jnp.max(s, axis=-1, keepdims=True)
    e = jnp.exp(s - peak)
    p = e / jnp.sum(e, axis=-1, keepdims=True)
    p_low = p.astype(jnp.bfloat16)
    o = jnp.einsum("mhgij,mjhd->mihgd", p_low, v, preferred_element_type=jnp.float32)
    return p, p_low, o.astype(jnp.bfloat16)


def layer_pass(x_low, dy, which, position, layer):
    wq, wk, wv, wo, wg, wu, wd, gain1, gain2 = layer
    rows = x_low.shape[0]
    group = QUERY_HEADS // KEY_VALUE_HEADS
    scale = HEAD_WIDTH ** (-0.5)
    gain1 = gain1.astype(jnp.float32)
    gain2 = gain2.astype(jnp.float32)
    x = x_low.astype(jnp.float32)
    r1 = lax.rsqrt(jnp.mean(x * x, axis=-1, keepdims=True) + eps_norm)
    n1 = x * r1
    a1 = (n1 * gain1).astype(jnp.bfloat16)
    cos, sin = rope_tables(position)
    q = rotate(nn(a1, wq).reshape(rows, QUERY_HEADS, HEAD_WIDTH), cos, sin).astype(jnp.bfloat16)
    k = rotate(nn(a1, wk).reshape(rows, KEY_VALUE_HEADS, HEAD_WIDTH), cos, sin).astype(jnp.bfloat16)
    v = nn(a1, wv).astype(jnp.bfloat16)
    q = q.reshape(MB, WIN, KEY_VALUE_HEADS, group, HEAD_WIDTH)
    k = k.reshape(MB, WIN, KEY_VALUE_HEADS, HEAD_WIDTH)
    v = v.reshape(MB, WIN, KEY_VALUE_HEADS, HEAD_WIDTH)
    seg = which.reshape(MB, WIN)
    ids = jnp.arange(WIN, dtype=jnp.int32)
    allowed = (seg[:, :, None] == seg[:, None, :]) & (ids[None, :] <= ids[:, None])[None]
    allowed = allowed[:, None, None]
    p, p_low, o = attention_forward(q, k, v, allowed)
    o = o.reshape(rows, QW)
    x2 = x + nn(o, wo)
    r2 = lax.rsqrt(jnp.mean(x2 * x2, axis=-1, keepdims=True) + eps_norm)
    n2 = x2 * r2
    a2 = (n2 * gain2).astype(jnp.bfloat16)
    g = nn(a2, wg)
    u = nn(a2, wu)
    sig = jax.nn.sigmoid(g)
    sw = g * sig
    hid = (sw * u).astype(jnp.bfloat16)
    block_rows = (x2 + nn(hid, wd)).astype(jnp.bfloat16)

    dhid = nt(dy, wd)
    dg = (dhid * u * sig * (1.0 + g * (1.0 - sig))).astype(jnp.bfloat16)
    du = (dhid * sw).astype(jnp.bfloat16)
    da2 = nt(dg, wg) + nt(du, wu)
    g_gain2 = jnp.sum(da2 * n2, axis=0)
    e2 = da2 * gain2
    dx2 = dy.astype(jnp.float32) + r2 * (e2 - n2 * jnp.mean(e2 * n2, axis=-1, keepdims=True))
    dat = dx2.astype(jnp.bfloat16)
    do = nt(dat, wo).astype(jnp.bfloat16).reshape(MB, WIN, KEY_VALUE_HEADS, group, HEAD_WIDTH)
    dp = jnp.einsum("mihgd,mjhd->mhgij", do, v, preferred_element_type=jnp.float32)
    spread = jnp.sum(p * dp, axis=-1, keepdims=True)
    ds = (p * (dp - spread)).astype(jnp.bfloat16)
    dq = jnp.einsum("mhgij,mjhd->mihgd", ds, k, preferred_element_type=jnp.float32) * scale
    dk = jnp.einsum("mhgij,mihgd->mjhd", ds, q, preferred_element_type=jnp.float32) * scale
    dv = jnp.einsum("mhgij,mihgd->mjhd", p_low, do, preferred_element_type=jnp.float32)
    dqf = rotate(dq.reshape(rows, QUERY_HEADS, HEAD_WIDTH), cos, -sin).reshape(rows, QW).astype(jnp.bfloat16)
    dkf = rotate(dk.reshape(rows, KEY_VALUE_HEADS, HEAD_WIDTH), cos, -sin).reshape(rows, KVW).astype(jnp.bfloat16)
    dvf = dv.reshape(rows, KVW).astype(jnp.bfloat16)
    da1 = nt(dqf, wq) + nt(dkf, wk) + nt(dvf, wv)
    g_gain1 = jnp.sum(da1 * n1, axis=0)
    e1 = da1 * gain1
    dx = dx2 + r1 * (e1 - n1 * jnp.mean(e1 * n1, axis=-1, keepdims=True))
    lefts = (a1, o, a2, hid)
    rights = (dqf, jnp.concatenate([dkf, dvf], axis=1), dat, dg, du)
    return block_rows, dx.astype(jnp.bfloat16), lefts, rights, (g_gain1, g_gain2)


def body(
    tokens,
    query_weight,
    key_weight,
    value_weight,
    out_weight,
    gate_weight,
    up_weight,
    down_weight,
    attention_gain,
    feedforward_gain,
    lengths,
    deal,
    block_cotangent,
):
    me = lax.axis_index("shard")
    core = me % 2
    gains = jnp.pad(jnp.stack([attention_gain, feedforward_gain]), ((0, 0), (0, 32))).reshape(1, 256)
    gains = jnp.pad(gains, ((0, 15), (0, 0)))
    parts = (
        query_weight,
        key_weight,
        value_weight,
        out_weight,
        gate_weight,
        up_weight,
        down_weight,
        gains,
    )
    full, halo = gather_weights(parts, tokens, block_cotangent)
    gains_full = full[7].reshape(SHARDS, 16, 2, 128)[:, 0, :, :96]
    layer = (*full[:7], gains_full[:, 0].reshape(D), gains_full[:, 1].reshape(D))
    window = jnp.concatenate([jnp.stack([tokens, block_cotangent]), halo], axis=2)
    layout = [window_layout(lengths[m, 0], me * BIN) for m in range(MB)]
    which = jnp.concatenate([one[0] for one in layout])
    position = jnp.concatenate([one[1] for one in layout])
    mine = jnp.concatenate([one[2] for one in layout])
    window = jnp.where(mine[None, :, None], window.reshape(2, ROWS, D), 0)
    position = jnp.where(mine, position, 0)
    dy = window[1]
    block_rows, input_rows, lefts, rights, gain_grads = layer_pass(window[0], dy, which, position, layer)

    gain_rows = jnp.pad(jnp.stack(gain_grads), ((0, 14), (0, 0))).astype(jnp.bfloat16)
    arrays = (*lefts, gain_rows, *rights, dy)
    both = exchange(arrays, (True,) * 5 + (False,) * 6)
    a1, o, a2, hid, gain_both, dqf, dkv, dat, dg, du, dy = both
    pairs = ((a1, dqf), (a1, dkv), (o, dat), (a2, dg), (a2, du), (hid, dy))
    grads = [tn(left, right).astype(jnp.bfloat16) for left, right in pairs]
    grads = [grad.reshape(2, 4, -1, grad.shape[-1]) for grad in grads]
    gain_both = gain_both.astype(jnp.float32).reshape(2, 16, D)
    gain_sum = (gain_both[0, :2] + gain_both[1, :2]).reshape(2, 2, 4, 192).transpose(1, 2, 0, 3)
    gain_sum = jnp.pad(gain_sum, ((0, 0), (0, 0), (0, 62), (0, 64))).astype(jnp.bfloat16)
    totals, gain_totals, from_before = reduce_grads(
        (*grads, gain_sum), block_rows.reshape(MB, WIN, D), input_rows.reshape(MB, WIN, D)
    )

    results = jnp.stack([block_rows, input_rows]).reshape(2, MB, WIN, D)[:, :, :BIN]
    from_before = jnp.pad(from_before, ((0, 0), (0, 0), (0, BIN - HALO), (0, 0)))
    mine_own = jnp.stack([one[2][:BIN] for one in layout])[None, :, :, None]
    inside = jnp.stack([one[3][:BIN] for one in layout])[None, :, :, None]
    rows_out = jnp.where(mine_own, results, jnp.where(inside, from_before, 0))
    g_query, g_kv, g_out, g_gate, g_up, g_down = [total.astype(jnp.float32) for total in totals]
    gain_out = lax.dynamic_slice_in_dim(gain_totals[:2].astype(jnp.float32), core * 96, 96, axis=1)
    return (
        rows_out[0],
        rows_out[1],
        g_query,
        g_kv[:, :KVW],
        g_kv[:, KVW:],
        g_out,
        g_gate,
        g_up,
        g_down,
        gain_out[0],
        gain_out[1],
    )


def solution(mesh):
    placed = (
        P(None, ("rep", "shard"), None),
        *([P("shard", None)] * 7),
        P("shard"),
        P("shard"),
        P(None, "rep", None),
        P(None, "rep", None),
        P(None, ("rep", "shard"), None),
    )
    return jax.shard_map(
        body,
        mesh=mesh,
        in_specs=placed,
        out_specs=(
            P(None, ("rep", "shard"), None),
            P(None, ("rep", "shard"), None),
            *([P("shard", None)] * 7),
            P("shard"),
            P("shard"),
        ),
        check_vma=False,
    )
```

```python
import math

import jax
import jax.numpy as jnp
from jax import lax
from jax.experimental import pallas as pl
from jax.experimental.pallas import tpu as pltpu
from jax.sharding import PartitionSpec as P

D = 1536
QUERY_HEADS = 16
KEY_VALUE_HEADS = 8
HEAD_WIDTH = 96
QW = QUERY_HEADS * HEAD_WIDTH
KVW = KEY_VALUE_HEADS * HEAD_WIDTH
FF = 4096
BIN = 64
HALO = 48
WIN = BIN + HALO
MB = 2
SHARDS = 16
ROWS = MB * WIN
MESH = pl.DeviceIdType.MESH
ANY = pl.BlockSpec(memory_space=pl.ANY)
DMA = pltpu.SemaphoreType.DMA

eps_norm = 1e-05
rope_base = 100000.0


class Place:
    def __init__(self):
        rep, shard = lax.axis_index("rep"), lax.axis_index("shard")
        self.rep, self.shard = rep, shard
        self.x, self.yl = rep // 2, rep % 2
        self.yh, self.z, self.c = shard // 8, (shard // 2) % 4, shard % 2
        self.y = self.yh * 2 + self.yl
        self.half = jnp.where(self.yh == self.yl, 1, 0)

    def at(self, x=None, yh=None, yl=None, z=None, c=None):
        def pick(new, old):
            return old if new is None else new

        rep = pick(x, self.x) * 2 + pick(yl, self.yl)
        return rep, pick(yh, self.yh) * 8 + pick(z, self.z) * 2 + pick(c, self.c)

    def along(self, dim):
        found = []
        for o in (1, 2, 3):
            x, yh, yl, z = self.x, self.yh, self.yl, self.z
            if dim == "x":
                x = (x + o) % 4
            elif dim == "z":
                z = (z + o) % 4
            else:
                y = (self.y + o) % 4
                yh, yl = y // 2, y % 2
            found.append((x, yh, yl, z))
        return found

    def peers(self, dim):
        return [self.at(*where) for where in self.along(dim)]

    def cross(self):
        return self.at(yh=1 - self.yh, yl=1 - self.yl)

    def inner(self):
        return self.at(yl=1 - self.yl)

    def sibling(self):
        return self.at(c=1 - self.c)

    def step(self, by):
        return self.rep, (self.shard + by + SHARDS) % SHARDS


def meet(peers):
    barrier = pltpu.get_barrier_semaphore()
    for peer in peers:
        pl.semaphore_signal(barrier, inc=1, device_id=peer, device_id_type=MESH)
    pl.semaphore_wait(barrier, len(peers))


class Sender:
    def __init__(self):
        self.pending = []

    def __call__(self, src, dst, send_sem, recv_sem, to):
        copy = pltpu.make_async_remote_copy(
            src_ref=src,
            dst_ref=dst,
            send_sem=send_sem,
            recv_sem=recv_sem,
            device_id=to,
            device_id_type=MESH,
        )
        copy.start()
        self.pending.append(copy)
        return copy

    def drain(self):
        for copy in self.pending:
            copy.wait_send()


def cut(first, count):
    if isinstance(first, int):
        return pl.ds(first, count)
    return pl.ds(pl.multiple_of(first, 128), count)


def rcut(first, count):
    if isinstance(first, int):
        return pl.ds(first, count)
    return pl.ds(pl.multiple_of(first, 16), count)


GATHER_UNITS = [(7, 0, 256, False), (1, 0, 768, False), (2, 0, 768, False)]
GATHER_UNITS += [(a, i * 768, 768, False) for a in (0, 3) for i in range(2)]
GATHER_UNITS += [(4, 0, 512, True), (4, 2048, 512, True), (5, 0, 512, True)]
GATHER_UNITS += [(6, i * 256, 256, False) for i in range(6)] + [(5, 2048 + i * 512, 512, False) for i in range(4)]
AHEAD = 3


def gather_kernel(*refs):
    ins, rows_in, outs, halo = refs[:8], refs[8:10], refs[10:18], refs[18]
    z_send, z_recv, y_send, y_recv, s_send, s_recv, x_send, x_recv, h_send, h_recv, local_sem = refs[19:30]
    staged = refs[30:]
    me = Place()
    units = GATHER_UNITS
    local, z_sent, y_one, y_two, x_sent, s_sent = {}, {}, {}, {}, {}, []

    def columns(u, half=None, quarter=None):
        array, first, count, over_x = units[u]
        if over_x:
            first = first + (me.x if quarter is None else quarter) * count
        if half is None:
            return cut(first, count)
        return cut(first + half * (count // 2), count // 2)

    count = len(units)
    for u in range(count):
        local[u] = pltpu.make_async_copy(ins[units[u][0]].at[:, columns(u)], staged[u], local_sem.at[u, 0])
        local[u].start()
    meet(me.peers("z") + me.peers("x") + [me.cross(), me.inner(), me.sibling(), me.step(-1), me.step(1)])
    send = Sender()

    def to_sibling(u, at, ref):
        s_sent.append(send(ref, ref, s_send.at[u, at], s_recv.at[u, at], me.sibling()))

    def z_phase(u):
        a = units[u][0]
        src, dst = ins[a].at[:, columns(u)], outs[a].at[me.yh, me.z, me.c, :, columns(u)]
        z_sent[u] = [send(src, dst, z_send.at[u, i], z_recv.at[u, i], to) for i, to in enumerate(me.peers("z"))]
        local[u].wait()
        local[u] = pltpu.make_async_copy(staged[u], dst, local_sem.at[u, 1])
        local[u].start()

    def y_phase(u):
        a = units[u][0]
        local[u].wait()
        for copy in z_sent[u]:
            copy.wait_recv()
        ref = outs[a].at[me.yh, :, me.c, :, columns(u, me.half)]
        y_one[u] = send(ref, ref, y_send.at[u, 0], y_recv.at[u, 0], me.cross())
        if not units[u][3]:
            to_sibling(u, 0, outs[a].at[me.yh, :, me.c, :, columns(u)])

    def forward_phase(u):
        a = units[u][0]
        y_one[u].wait_recv()
        ref = outs[a].at[1 - me.yh, :, me.c, :, columns(u, me.half)]
        y_two[u] = send(ref, ref, y_send.at[u, 1], y_recv.at[u, 1], me.inner())

    def last_phase(u):
        a = units[u][0]
        y_two[u].wait_recv()
        if units[u][3]:
            ref = outs[a].at[:, :, me.c, :, columns(u)]
            x_sent[u] = [send(ref, ref, x_send.at[u, i], x_recv.at[u, i], to) for i, to in enumerate(me.peers("x"))]
            to_sibling(u, 3, ref)
        else:
            to_sibling(u, 1, outs[a].at[1 - me.yh, :, me.c, :, columns(u)])

    for i, src in enumerate(rows_in):
        s_sent.append(send(src.at[:, pl.ds(0, HALO)], halo.at[i], h_send.at[i], h_recv.at[i], me.step(-1)))
    for u in range(AHEAD):
        z_phase(u)
    for t in range(count + 2):
        if t + AHEAD < count:
            z_phase(t + AHEAD)
        if t < count:
            y_phase(t)
        if 1 <= t <= count:
            forward_phase(t - 1)
        if t >= 2:
            last_phase(t - 2)
    for u in x_sent:
        for i in range(3):
            x_sent[u][i].wait_recv()
            to_sibling(u, i, outs[units[u][0]].at[:, :, me.c, :, columns(u, None, (me.x + 3 - i) % 4)])
    for copy in s_sent:
        copy.wait_recv()
    send.drain()


def gather_weights(parts, tokens, cotangent):
    count = len(GATHER_UNITS)
    outs = [jax.ShapeDtypeStruct((2, 4, 2, *part.shape), part.dtype) for part in parts]
    outs.append(jax.ShapeDtypeStruct((2, MB, HALO, D), jnp.bfloat16))
    results = pl.pallas_call(
        gather_kernel,
        out_shape=outs,
        in_specs=[ANY] * 10,
        out_specs=[ANY] * 9,
        scratch_shapes=[DMA((count, 3))] * 2 + [DMA((count, 2))] * 2 + [DMA((count, 4))] * 2 + [DMA((count, 3))] * 2
        + [DMA((2,))] * 2 + [DMA((count, 2))]
        + [pltpu.VMEM((parts[a].shape[0], n), jnp.bfloat16) for a, _, n, _ in GATHER_UNITS],
        compiler_params=pltpu.CompilerParams(collective_id=1, has_side_effects=True, vmem_limit_bytes=16 * 2**20),
        name="gather_weights",
    )(*parts, tokens, cotangent)
    return [full.reshape(-1, full.shape[-1]) for full in results[:8]], results[8]


def exchange_kernel(whole, *refs):
    count = len(whole)
    ins, outs = refs[:count], refs[count : 2 * count]
    send_sem, recv_sem, local_sem = refs[2 * count : 2 * count + 3]
    staged = refs[2 * count + 3 :]
    me = Place()
    local = []
    for i, (src, dst) in enumerate(zip(ins, outs)):
        width = dst.shape[-1]
        own = src if whole[i] else src.at[:, cut(me.c * width, width)]
        local.append(pltpu.make_async_copy(own, staged[i], local_sem.at[i, 0]))
        local[i].start()
    meet([me.sibling()])
    send = Sender()
    for i, (src, dst) in enumerate(zip(ins, outs)):
        width = dst.shape[-1]
        theirs = src if whole[i] else src.at[:, cut((1 - me.c) * width, width)]
        send(theirs, dst.at[me.c], send_sem.at[i], recv_sem.at[i], me.sibling())
    for i, dst in enumerate(outs):
        local[i].wait()
        local[i] = pltpu.make_async_copy(staged[i], dst.at[me.c], local_sem.at[i, 1])
        local[i].start()
    for i, copy in enumerate(send.pending):
        local[i].wait()
        copy.wait_recv()
    send.drain()


def exchange(arrays, whole):
    count = len(arrays)
    outs = []
    for array, full in zip(arrays, whole):
        rows, width = array.shape
        outs.append(jax.ShapeDtypeStruct((2, rows, width if full else width // 2), array.dtype))
    results = pl.pallas_call(
        lambda *refs: exchange_kernel(whole, *refs),
        out_shape=outs,
        in_specs=[ANY] * count,
        out_specs=[ANY] * count,
        scratch_shapes=[DMA((count,))] * 2 + [DMA((count, 2))] + [pltpu.VMEM(out.shape[1:], out.dtype) for out in outs],
        compiler_params=pltpu.CompilerParams(collective_id=2, has_side_effects=True, vmem_limit_bytes=24 * 2**20),
        name="exchange_rows",
    )(*arrays)
    return [both.reshape(-1, both.shape[-1]) for both in results]


REDUCE_ROWS = (192, 192, 192, 192, 192, 512, 64)
REDUCE_COLUMNS = (768, 768, 768, 2048, 2048, 768, 256)
REDUCE_DIMS = {"A": "zyx", "B": "yxz", "C": "xzy"}
REDUCE_UNITS = [("A", 3, i * 512, 512) for i in range(4)] + [("A", 0, 0, 768)]
REDUCE_UNITS += [("B", 4, i * 512, 512) for i in range(4)] + [("B", 1, 0, 768)]
REDUCE_UNITS += [("C", 5, i * 256, 256) for i in range(3)] + [("C", 2, 0, 768), ("C", 6, 0, 256)]
ROUNDS = [(t, 5 + t, 10 + t) for t in range(5)]
GAINS = 6


def reduce_shapes(u):
    order, a, _, n = REDUCE_UNITS[u]
    r = REDUCE_ROWS[a]
    first = {"A": (2, r, n), "B": (4, r, n // 2), "C": (2, 4, r // 4, n)}[order]
    second = {"A": (r, n // 2), "B": (4, r // 4, n // 2), "C": (2, r // 4, n)}[order]
    return first, second, (r // 4, n // 2)


def add_into(total, parts):
    *lead, rows, _ = total.shape
    blocks = rows // 16

    def step(i, carry):
        where, rest = [], i // blocks
        for n in reversed(lead):
            where.insert(0, rest % n)
            rest = rest // n
        where = (*where, rcut((i % blocks) * 16, 16), slice(None))
        s = total[where].astype(jnp.float32)
        for k in range(3):
            s = s + parts[(k, *where)].astype(jnp.float32)
        total[where] = s.astype(jnp.bfloat16)
        return carry

    lax.fori_loop(0, math.prod(lead) * blocks, step, 0)


def reduce_kernel(*refs):
    nu = len(REDUCE_UNITS)
    ins, rows_in, outs, halo, totals = refs[:7], refs[7:9], refs[9:16], refs[16], refs[17:24]
    rest = refs[24:]
    kept = (rest[:nu], rest[nu : 2 * nu], rest[2 * nu : 3 * nu])
    taken = (rest[3 * nu : 4 * nu], rest[4 * nu : 5 * nu], rest[5 * nu : 6 * nu])
    send_sem, recv_sem, g_send, g_recv, s_send, s_recv, h_send, h_recv, local_sem, final_sem = rest[6 * nu :]
    me = Place()
    meet(me.peers("z") + me.peers("x") + me.peers("y") + [me.sibling(), me.step(-1), me.step(1)])
    send = Sender()
    sent, own = {}, {}

    def share(u, stage, x, yh, yl, z):
        order, a, first, n = REDUCE_UNITS[u]
        r = REDUCE_ROWS[a] // 4
        src = ins[a] if stage == 0 else kept[stage - 1][u]
        begin = first if stage == 0 else 0
        dim = REDUCE_DIMS[order][stage]
        lead = {"A": 2, "B": 2, "C": 2}[order] if stage == 0 else len(src.shape) - 2
        columns = slice(None) if stage else cut(begin, n)
        if dim == "z":
            return src.at[:, z, :, columns] if lead == 2 else src.at[z]
        if dim == "x":
            rows = rcut(x * r, r)
            if lead == 2:
                return src.at[:, :, rows, columns]
            return src.at[:, rows] if lead == 1 else src.at[rows]
        columns = cut(begin + yl * (n // 2), n // 2)
        if lead == 2:
            return src.at[yh, :, :, columns]
        return src.at[yh, :, columns]

    def issue(u, stage):
        dim = REDUCE_DIMS[REDUCE_UNITS[u][0]][stage]
        sent[u, stage] = [
            send(share(u, stage, *where), taken[stage][u].at[i], send_sem.at[u, stage, i], recv_sem.at[u, stage, i], me.at(*where))
            for i, where in enumerate(me.along(dim))
        ]
        own[u, stage] = pltpu.make_async_copy(
            share(u, stage, me.x, me.yh, me.yl, me.z), kept[stage][u], local_sem.at[u, stage]
        )
        own[u, stage].start()

    def finish(u, stage):
        own[u, stage].wait()
        for copy in sent[u, stage]:
            copy.wait_recv()
        add_into(kept[stage][u], taken[stage][u])

    def result(u, all_x, all_y):
        order, a, first, n = REDUCE_UNITS[u]
        r = REDUCE_ROWS[a] // 4
        rows = slice(None) if all_x else rcut(me.x * r, r)
        columns = cut(first, n) if all_y else cut(first + me.yl * (n // 2), n // 2)
        return totals[a].at[rows, columns]

    def spread_one(u):
        order = REDUCE_UNITS[u][0]
        dst = result(u, False, False)
        own[u, 3] = pltpu.make_async_copy(kept[2][u], dst, local_sem.at[u, 3])
        own[u, 3].start()
        to = [me.inner()] if order == "C" else me.peers("x")
        sent[u, 3] = [send(kept[2][u], dst, g_send.at[u, i], g_recv.at[u, i], one) for i, one in enumerate(to)]

    def spread_two(u):
        order = REDUCE_UNITS[u][0]
        own[u, 3].wait()
        for copy in sent[u, 3]:
            copy.wait_recv()
        ref = result(u, order != "C", order == "C")
        to = me.peers("x") if order == "C" else [me.inner()]
        sent[u, 4] = [send(ref, ref, g_send.at[u, 3 + i], g_recv.at[u, 3 + i], one) for i, one in enumerate(to)]

    last = []

    def deliver(u):
        order, a, first, n = REDUCE_UNITS[u]
        for copy in sent[u, 4]:
            copy.wait_recv()
        if a == GAINS:
            own[u, 5] = pltpu.make_async_copy(totals[a], outs[a], final_sem.at[u])
            own[u, 5].start()
            return
        r, width = REDUCE_ROWS[a] // 2, REDUCE_COLUMNS[a]
        dst = outs[a].at[:, cut(me.c * width + first, n)]
        last.append(send(totals[a].at[rcut((1 - me.c) * r, r), cut(first, n)], dst, s_send.at[u], s_recv.at[u], me.sibling()))
        own[u, 5] = pltpu.make_async_copy(totals[a].at[rcut(me.c * r, r), cut(first, n)], dst, final_sem.at[u])
        own[u, 5].start()

    for i, src in enumerate(rows_in):
        last.append(send(src.at[:, pl.ds(BIN, HALO)], halo.at[i], h_send.at[i], h_recv.at[i], me.step(1)))
    count = len(ROUNDS)
    for u in ROUNDS[0]:
        issue(u, 0)
    for t in range(count + 4):
        if t + 1 < count:
            for u in ROUNDS[t + 1]:
                issue(u, 0)
        for stage in range(2):
            if 0 <= t - stage < count:
                for u in ROUNDS[t - stage]:
                    finish(u, stage)
                    issue(u, stage + 1)
        if 0 <= t - 2 < count:
            for u in ROUNDS[t - 2]:
                finish(u, 2)
                spread_one(u)
        if 0 <= t - 3 < count:
            for u in ROUNDS[t - 3]:
                spread_two(u)
        if 0 <= t - 4 < count:
            for u in ROUNDS[t - 4]:
                deliver(u)
    for u in range(nu):
        own[u, 5].wait()
    for copy in last:
        copy.wait_recv()
    send.drain()


def reduce_grads(grads, block_rows, input_rows):
    nu = len(REDUCE_UNITS)
    first, second, third = zip(*[reduce_shapes(u) for u in range(nu)])
    low = jnp.bfloat16
    shapes = list(zip(REDUCE_ROWS, REDUCE_COLUMNS))
    outs = [jax.ShapeDtypeStruct((r // 2, 2 * n), low) for r, n in shapes[:GAINS]]
    outs.append(jax.ShapeDtypeStruct(shapes[GAINS], low))
    outs.append(jax.ShapeDtypeStruct((2, MB, HALO, D), low))
    scratch = [pltpu.VMEM(s, low) for s in shapes]
    scratch += [pltpu.VMEM(s, low) for s in (*first, *second, *third)]
    scratch += [pltpu.VMEM((3, *s), low) for s in (*first, *second, *third)]
    scratch += [DMA((nu, 3, 3))] * 2 + [DMA((nu, 6))] * 2 + [DMA((nu,))] * 2 + [DMA((2,))] * 2 + [DMA((nu, 4)), DMA((nu,))]
    results = pl.pallas_call(
        reduce_kernel,
        out_shape=outs,
        in_specs=[ANY] * 9,
        out_specs=[ANY] * len(outs),
        scratch_shapes=scratch,
        compiler_params=pltpu.CompilerParams(collective_id=3, has_side_effects=True, vmem_limit_bytes=56 * 2**20),
        name="reduce_grads",
    )(*grads, block_rows, input_rows)
    return results[:GAINS], results[GAINS], results[GAINS + 1]


def window_layout(seq_lengths, first_row):
    count = seq_lengths.shape[0]
    ids = jnp.arange(count, dtype=jnp.int32)
    earlier = ids[None, :] < ids[:, None]
    start = jnp.sum(jnp.where(earlier, seq_lengths[None, :], 0), axis=1)
    end = start + seq_lengths
    rows = first_row + jnp.arange(WIN, dtype=jnp.int32)
    which = jnp.sum((rows[:, None] >= end[None, :]).astype(jnp.int32), axis=1)
    onehot = which[:, None] == ids[None, :]
    begin = jnp.sum(jnp.where(onehot, start[None, :], 0), axis=1)
    inside = which < count
    mine = inside & (begin >= first_row) & (begin < first_row + BIN)
    return which, rows - begin, mine, inside


def dot(a, b, dims):
    return lax.dot_general(a, b, (dims, ((), ())), preferred_element_type=jnp.float32)


def nn(a, b):
    return dot(a, b, ((1,), (0,)))


def nt(a, b):
    return dot(a, b, ((1,), (1,)))


def tn(a, b):
    return dot(a, b, ((0,), (0,)))


FF_BLOCK = 512
FF_BLOCKS = FF // FF_BLOCK
CHUNK = 4 * HEAD_WIDTH
SCALE = HEAD_WIDTH ** (-0.5)


def mean_of(value):
    return jnp.mean(value, axis=-1, keepdims=True)


def swap_halves(value):
    lane = lax.broadcasted_iota(jnp.int32, value.shape, 1) % HEAD_WIDTH
    return jnp.where(
        lane < HEAD_WIDTH // 2, pltpu.roll(value, CHUNK - HEAD_WIDTH // 2, 1), pltpu.roll(value, HEAD_WIDTH // 2, 1)
    )


def split_heads(dst, chunk, value):
    for i in range(4):
        dst[4 * chunk + i, :, :HEAD_WIDTH] = value[:, HEAD_WIDTH * i : HEAD_WIDTH * (i + 1)].astype(jnp.bfloat16)


def attention_forward(x_ref, gain_ref, cos_ref, sin_ref, seg_ref, segt_ref, wq, wk, wv, wo, a1_ref, o_ref, q_ref, k_ref, v_ref, x2_ref):
    x = x_ref[...].astype(jnp.float32)
    r1 = lax.rsqrt(mean_of(x * x) + eps_norm)
    a1_ref[...] = (x * r1 * gain_ref[...]).astype(jnp.bfloat16)
    cos, sin = cos_ref[...], sin_ref[...]
    for ref in (q_ref, k_ref, v_ref):
        ref[:, :, HEAD_WIDTH:] = jnp.zeros((ref.shape[0], ROWS, 128 - HEAD_WIDTH), jnp.bfloat16)
    for weight, dst, turned in ((wq, q_ref, True), (wk, k_ref, True), (wv, v_ref, False)):
        for chunk in range(weight.shape[1] // CHUNK):
            value = nn(a1_ref[...], weight[:, CHUNK * chunk : CHUNK * (chunk + 1)])
            if turned:
                value = value * cos + swap_halves(value) * sin
            split_heads(dst, chunk, value)
    allowed = allowed_pairs(seg_ref, segt_ref)
    for head in range(QUERY_HEADS):
        p = probabilities(q_ref[head], k_ref[head // 2], allowed)
        o = nn(p.astype(jnp.bfloat16), v_ref[head // 2])
        o_ref[:, HEAD_WIDTH * head : HEAD_WIDTH * (head + 1)] = o[:, :HEAD_WIDTH].astype(jnp.bfloat16)
    x2_ref[...] = x + nn(o_ref[...], wo[...])


def allowed_pairs(seg_ref, segt_ref):
    row = lax.broadcasted_iota(jnp.int32, (ROWS, ROWS), 0)
    column = lax.broadcasted_iota(jnp.int32, (ROWS, ROWS), 1)
    return (seg_ref[...] == segt_ref[...]) & (column <= row)


def probabilities(q, k, allowed):
    s = jnp.where(allowed, nt(q, k) * SCALE, -1e30)
    e = jnp.exp(s - jnp.max(s, axis=-1, keepdims=True))
    return e / jnp.sum(e, axis=-1, keepdims=True)


def second_norm(x2_ref, gain_ref, a2_ref):
    x2 = x2_ref[...]
    r2 = lax.rsqrt(mean_of(x2 * x2) + eps_norm)
    a2_ref[...] = (x2 * r2 * gain_ref[...]).astype(jnp.bfloat16)


def feedforward_block(first, a2_ref, dy_ref, wg, wu, wd, hid_ref, dg_ref, du_ref, yb_ref, da2_ref):
    at = cut(first, FF_BLOCK)
    g = nn(a2_ref[...], wg[...])
    u = nn(a2_ref[...], wu[...])
    sig = jax.nn.sigmoid(g)
    sw = g * sig
    hid = (sw * u).astype(jnp.bfloat16)
    hid_ref[:, at] = hid
    dhid = nt(dy_ref[...], wd[...])
    dg = (dhid * u * sig * (1.0 + g * (1.0 - sig))).astype(jnp.bfloat16)
    du = (dhid * sw).astype(jnp.bfloat16)
    dg_ref[:, at] = dg
    du_ref[:, at] = du
    yb_ref[...] += nn(hid, wd[...])
    da2_ref[...] += nt(dg, wg[...]) + nt(du, wu[...])


def feedforward_back(dy_ref, x2_ref, da2_ref, gain_ref, dat_ref, dgain_ref):
    x2, da2 = x2_ref[...], da2_ref[...]
    r2 = lax.rsqrt(mean_of(x2 * x2) + eps_norm)
    n2 = x2 * r2
    dgain_ref[1:2, :] = jnp.sum(da2 * n2, axis=0, keepdims=True)
    e2 = da2 * gain_ref[...]
    dx2 = dy_ref[...].astype(jnp.float32) + r2 * (e2 - n2 * mean_of(e2 * n2))
    da2_ref[...] = dx2
    dat_ref[...] = dx2.astype(jnp.bfloat16)


def attention_backward(
    x_ref, gain_ref, cos_ref, sin_ref, seg_ref, segt_ref, wq, wk, wv, wo, q_ref, k_ref, v_ref, dat_ref, dx2_ref, do_ref, turn_ref, dqf_ref, dkv_ref, dx_ref, dgain_ref
):
    do_ref[:, :, HEAD_WIDTH:] = jnp.zeros((QUERY_HEADS, ROWS, 128 - HEAD_WIDTH), jnp.bfloat16)
    for chunk in range(4):
        split_heads(do_ref, chunk, nt(dat_ref[...], wo[CHUNK * chunk : CHUNK * (chunk + 1), :]))
    allowed = allowed_pairs(seg_ref, segt_ref)
    for c in range(KEY_VALUE_HEADS):
        k, v = k_ref[c], v_ref[c]
        dk = jnp.zeros((ROWS, 128), jnp.float32)
        dv = jnp.zeros((ROWS, 128), jnp.float32)
        for head in (2 * c, 2 * c + 1):
            q, do = q_ref[head], do_ref[head]
            p = probabilities(q, k, allowed)
            dp = nt(do, v)
            ds = (p * (dp - jnp.sum(p * dp, axis=-1, keepdims=True))).astype(jnp.bfloat16)
            dq = nn(ds, k) * SCALE
            turn_ref[:, HEAD_WIDTH * head : HEAD_WIDTH * (head + 1)] = dq[:, :HEAD_WIDTH]
            dk = dk + tn(ds, q)
            dv = dv + tn(p.astype(jnp.bfloat16), do)
        dkv_ref[:, KVW + HEAD_WIDTH * c : KVW + HEAD_WIDTH * (c + 1)] = dv[:, :HEAD_WIDTH].astype(jnp.bfloat16)
        turn_ref[:, QW + HEAD_WIDTH * c : QW + HEAD_WIDTH * (c + 1)] = (dk * SCALE)[:, :HEAD_WIDTH]
    cos, sin = cos_ref[...], sin_ref[...]
    for chunk in range(6):
        value = turn_ref[:, CHUNK * chunk : CHUNK * (chunk + 1)]
        value = (value * cos - swap_halves(value) * sin).astype(jnp.bfloat16)
        if chunk < 4:
            dqf_ref[:, CHUNK * chunk : CHUNK * (chunk + 1)] = value
        else:
            dkv_ref[:, CHUNK * (chunk - 4) : CHUNK * (chunk - 3)] = value
    da1 = nt(dqf_ref[...], wq[...]) + nt(dkv_ref[:, :KVW], wk[...]) + nt(dkv_ref[:, KVW:], wv[...])
    x = x_ref[...].astype(jnp.float32)
    r1 = lax.rsqrt(mean_of(x * x) + eps_norm)
    n1 = x * r1
    dgain_ref[0:1, :] = jnp.sum(da1 * n1, axis=0, keepdims=True)
    e1 = da1 * gain_ref[...]
    dx = dx2_ref[...] + r1 * (e1 - n1 * mean_of(e1 * n1))
    dx_ref[...] = dx.astype(jnp.bfloat16)


def layer_kernel(
    x_ref, dy_ref, gain1_ref, gain2_ref, cos_ref, sin_ref, seg_ref, segt_ref, wq_hbm, wk_hbm, wv_hbm, wo_hbm, wg_hbm, wu_hbm, wd_hbm,
    block_ref, dx_ref, a1_ref, o_ref, a2_ref, hid_ref, dqf_ref, dkv_ref, dat_ref, dg_ref, du_ref, dgain_ref,
    wq, wk, wv, wo, wg, wu, wd, q_ref, k_ref, v_ref, do_ref, x2_ref, da2_ref, turn_ref, attention_sem, block_sem,
):
    loads = [
        pltpu.make_async_copy(src, dst, attention_sem.at[i])
        for i, (src, dst) in enumerate(((wq_hbm, wq), (wk_hbm, wk), (wv_hbm, wv), (wo_hbm, wo)))
    ]
    for load in loads:
        load.start()

    def block_loads(block, slot):
        first = block * FF_BLOCK
        return [
            pltpu.make_async_copy(wg_hbm.at[:, cut(first, FF_BLOCK)], wg.at[slot], block_sem.at[slot, 0]),
            pltpu.make_async_copy(wu_hbm.at[:, cut(first, FF_BLOCK)], wu.at[slot], block_sem.at[slot, 1]),
            pltpu.make_async_copy(wd_hbm.at[cut(first, FF_BLOCK), :], wd.at[slot], block_sem.at[slot, 2]),
        ]

    for load in block_loads(0, 0):
        load.start()
    for load in loads:
        load.wait()
    shared = (cos_ref, sin_ref, seg_ref, segt_ref, wq, wk, wv, wo)
    attention_forward(x_ref, gain1_ref, *shared, a1_ref, o_ref, q_ref, k_ref, v_ref, x2_ref)
    second_norm(x2_ref, gain2_ref, a2_ref)
    yb_ref = turn_ref.at[:, :D]
    yb_ref[...] = x2_ref[...]
    da2_ref[...] = jnp.zeros_like(da2_ref)

    def step(block, carry):
        slot = block % 2

        @pl.when(block + 1 < FF_BLOCKS)
        def _():
            for load in block_loads(block + 1, 1 - slot):
                load.start()

        for load in block_loads(block, slot):
            load.wait()
        feedforward_block(
            block * FF_BLOCK, a2_ref, dy_ref, wg.at[slot], wu.at[slot], wd.at[slot], hid_ref, dg_ref, du_ref, yb_ref, da2_ref
        )
        return carry

    lax.fori_loop(0, FF_BLOCKS, step, 0)
    block_ref[...] = yb_ref[...].astype(jnp.bfloat16)
    dgain_ref[...] = jnp.zeros_like(dgain_ref)
    feedforward_back(dy_ref, x2_ref, da2_ref, gain2_ref, dat_ref, dgain_ref)
    attention_backward(
        x_ref, gain1_ref, *shared, q_ref, k_ref, v_ref, dat_ref, da2_ref, do_ref, turn_ref, dqf_ref, dkv_ref, dx_ref, dgain_ref
    )


def layer_pass(x, dy, seg, position, layer):
    *weights, gain1, gain2 = layer
    low, full = jnp.bfloat16, jnp.float32
    half = HEAD_WIDTH // 2
    freq = jnp.exp(jnp.arange(half, dtype=full) * (-2.0 * math.log(rope_base) / HEAD_WIDTH))
    angle = position.astype(full)[:, None] * freq[None, :]
    cos, sin = jnp.cos(angle), jnp.sin(angle)
    cos = jnp.tile(cos, (1, 8))
    sin = jnp.tile(jnp.concatenate([-sin, sin], axis=1), (1, 4))
    wide = [(D, low), (D, low), (D, low), (QW, low), (D, low), (FF, low), (QW, low), (2 * KVW, low), (D, low), (FF, low), (FF, low)]
    outs = [jax.ShapeDtypeStruct((ROWS, n), t) for n, t in wide] + [jax.ShapeDtypeStruct((8, D), full)]
    vmem = pl.BlockSpec(memory_space=pltpu.VMEM)
    heads = [pltpu.VMEM((n, ROWS, 128), low) for n in (QUERY_HEADS, KEY_VALUE_HEADS, KEY_VALUE_HEADS, QUERY_HEADS)]
    scratch = [pltpu.VMEM(weight.shape, low) for weight in weights[:4]]
    scratch += [pltpu.VMEM((2, D, FF_BLOCK), low)] * 2 + [pltpu.VMEM((2, FF_BLOCK, D), low)] + heads
    scratch += [pltpu.VMEM((ROWS, D), full), pltpu.VMEM((ROWS, D), full), pltpu.VMEM((ROWS, QW + KVW), full), DMA((4,)), DMA((2, 3))]
    return pl.pallas_call(
        layer_kernel,
        out_shape=outs,
        in_specs=[vmem] * 8 + [ANY] * 7,
        out_specs=[vmem] * 12,
        scratch_shapes=scratch,
        compiler_params=pltpu.CompilerParams(vmem_limit_bytes=60 * 2**20),
        name="layer",
    )(x, dy, gain1.reshape(1, D), gain2.reshape(1, D), cos, sin, seg.reshape(ROWS, 1), seg.reshape(1, ROWS), *weights)


def body(
    tokens,
    query_weight,
    key_weight,
    value_weight,
    out_weight,
    gate_weight,
    up_weight,
    down_weight,
    attention_gain,
    feedforward_gain,
    lengths,
    deal,
    block_cotangent,
):
    me = lax.axis_index("shard")
    core = me % 2
    gains = jnp.pad(jnp.stack([attention_gain, feedforward_gain]), ((0, 0), (0, 32))).reshape(1, 256)
    gains = jnp.pad(gains, ((0, 15), (0, 0)))
    parts = (
        query_weight,
        key_weight,
        value_weight,
        out_weight,
        gate_weight,
        up_weight,
        down_weight,
        gains,
    )
    full, halo = gather_weights(parts, tokens, block_cotangent)
    gains_full = full[7].reshape(SHARDS, 16, 2, 128)[:, 0, :, :96]
    gains_full = gains_full.astype(jnp.float32)
    layer = (*full[:7], gains_full[:, 0], gains_full[:, 1])
    window = jnp.concatenate([jnp.stack([tokens, block_cotangent]), halo], axis=2)
    layout = [window_layout(lengths[m, 0], me * BIN) for m in range(MB)]
    seg = jnp.concatenate([one[0] + m * 64 for m, one in enumerate(layout)])
    position = jnp.concatenate([one[1] for one in layout])
    mine = jnp.concatenate([one[2] for one in layout])
    window = jnp.where(mine[None, :, None], window.reshape(2, ROWS, D), 0)
    position = jnp.where(mine, position, 0)
    dy = window[1]
    block_rows, input_rows, a1, o, a2, hid, dqf, dkv, dat, dg, du, dgain = layer_pass(window[0], dy, seg, position, layer)

    gain_rows = jnp.pad(dgain.astype(jnp.bfloat16), ((0, 8), (0, 0)))
    arrays = (a1, o, a2, hid, gain_rows, dqf, dkv, dat, dg, du, dy)
    both = exchange(arrays, (True,) * 5 + (False,) * 6)
    a1, o, a2, hid, gain_both, dqf, dkv, dat, dg, du, dy = both
    pairs = ((a1, dqf), (a1, dkv), (o, dat), (a2, dg), (a2, du), (hid, dy))
    grads = [tn(left, right).astype(jnp.bfloat16) for left, right in pairs]
    grads = [grad.reshape(2, 4, -1, grad.shape[-1]) for grad in grads]
    gain_both = gain_both.astype(jnp.float32).reshape(2, 16, D)
    gain_sum = (gain_both[0, :2] + gain_both[1, :2]).reshape(2, 2, 4, 192).transpose(1, 2, 0, 3)
    gain_sum = jnp.pad(gain_sum, ((0, 0), (0, 0), (0, 62), (0, 64))).astype(jnp.bfloat16)
    totals, gain_totals, from_before = reduce_grads(
        (*grads, gain_sum), block_rows.reshape(MB, WIN, D), input_rows.reshape(MB, WIN, D)
    )

    results = jnp.stack([block_rows, input_rows]).reshape(2, MB, WIN, D)[:, :, :BIN]
    from_before = jnp.pad(from_before, ((0, 0), (0, 0), (0, BIN - HALO), (0, 0)))
    mine_own = jnp.stack([one[2][:BIN] for one in layout])[None, :, :, None]
    inside = jnp.stack([one[3][:BIN] for one in layout])[None, :, :, None]
    rows_out = jnp.where(mine_own, results, jnp.where(inside, from_before, 0))
    g_query, g_kv, g_out, g_gate, g_up, g_down = [total.astype(jnp.float32) for total in totals]
    gain_out = lax.dynamic_slice_in_dim(gain_totals[:2].astype(jnp.float32), core * 96, 96, axis=1)
    return (
        rows_out[0],
        rows_out[1],
        g_query,
        g_kv[:, :KVW],
        g_kv[:, KVW:],
        g_out,
        g_gate,
        g_up,
        g_down,
        gain_out[0],
        gain_out[1],
    )


def solution(mesh):
    placed = (
        P(None, ("rep", "shard"), None),
        *([P("shard", None)] * 7),
        P("shard"),
        P("shard"),
        P(None, "rep", None),
        P(None, "rep", None),
        P(None, ("rep", "shard"), None),
    )
    return jax.shard_map(
        body,
        mesh=mesh,
        in_specs=placed,
        out_specs=(
            P(None, ("rep", "shard"), None),
            P(None, ("rep", "shard"), None),
            *([P("shard", None)] * 7),
            P("shard"),
            P("shard"),
        ),
        check_vma=False,
    )
```

```python
import math

import jax
import jax.numpy as jnp
from jax import lax
from jax.experimental import pallas as pl
from jax.experimental.pallas import tpu as pltpu
from jax.sharding import PartitionSpec as P

D = 1536
QUERY_HEADS = 16
KEY_VALUE_HEADS = 8
HEAD_WIDTH = 96
QW = QUERY_HEADS * HEAD_WIDTH
KVW = KEY_VALUE_HEADS * HEAD_WIDTH
FF = 4096
BIN = 64
HALO = 48
WIN = BIN + HALO
MB = 2
SHARDS = 16
ROWS = MB * WIN
MESH = pl.DeviceIdType.MESH
ANY = pl.BlockSpec(memory_space=pl.ANY)
DMA = pltpu.SemaphoreType.DMA

eps_norm = 1e-05
rope_base = 100000.0


class Place:
    def __init__(self):
        rep, shard = lax.axis_index("rep"), lax.axis_index("shard")
        self.rep, self.shard = rep, shard
        self.x, self.yl = rep // 2, rep % 2
        self.yh, self.z, self.c = shard // 8, (shard // 2) % 4, shard % 2
        self.y = self.yh * 2 + self.yl
        self.half = jnp.where(self.yh == self.yl, 1, 0)

    def at(self, x=None, yh=None, yl=None, z=None, c=None):
        def pick(new, old):
            return old if new is None else new

        rep = pick(x, self.x) * 2 + pick(yl, self.yl)
        return rep, pick(yh, self.yh) * 8 + pick(z, self.z) * 2 + pick(c, self.c)

    def along(self, dim):
        found = []
        for o in (1, 2, 3):
            x, yh, yl, z = self.x, self.yh, self.yl, self.z
            if dim == "x":
                x = (x + o) % 4
            elif dim == "z":
                z = (z + o) % 4
            else:
                y = (self.y + o) % 4
                yh, yl = y // 2, y % 2
            found.append((x, yh, yl, z))
        return found

    def peers(self, dim):
        return [self.at(*where) for where in self.along(dim)]

    def cross(self):
        return self.at(yh=1 - self.yh, yl=1 - self.yl)

    def inner(self):
        return self.at(yl=1 - self.yl)

    def sibling(self):
        return self.at(c=1 - self.c)

    def step(self, by):
        return self.rep, (self.shard + by + SHARDS) % SHARDS


def meet(peers):
    barrier = pltpu.get_barrier_semaphore()
    for peer in peers:
        pl.semaphore_signal(barrier, inc=1, device_id=peer, device_id_type=MESH)
    pl.semaphore_wait(barrier, len(peers))


class Sender:
    def __init__(self):
        self.pending = []

    def __call__(self, src, dst, send_sem, recv_sem, to):
        copy = pltpu.make_async_remote_copy(
            src_ref=src,
            dst_ref=dst,
            send_sem=send_sem,
            recv_sem=recv_sem,
            device_id=to,
            device_id_type=MESH,
        )
        copy.start()
        self.pending.append(copy)
        return copy

    def drain(self):
        for copy in self.pending:
            copy.wait_send()


def cut(first, count):
    if isinstance(first, int):
        return pl.ds(first, count)
    return pl.ds(pl.multiple_of(first, 128), count)


def rcut(first, count):
    if isinstance(first, int):
        return pl.ds(first, count)
    return pl.ds(pl.multiple_of(first, 16), count)


def exchange_kernel(whole, *refs):
    count = len(whole)
    ins, outs = refs[:count], refs[count : 2 * count]
    send_sem, recv_sem, local_sem = refs[2 * count : 2 * count + 3]
    staged = refs[2 * count + 3 :]
    me = Place()
    local = []
    for i, (src, dst) in enumerate(zip(ins, outs)):
        width = dst.shape[-1]
        own = src if whole[i] else src.at[:, cut(me.c * width, width)]
        local.append(pltpu.make_async_copy(own, staged[i], local_sem.at[i, 0]))
        local[i].start()
    meet([me.sibling()])
    send = Sender()
    for i, (src, dst) in enumerate(zip(ins, outs)):
        width = dst.shape[-1]
        theirs = src if whole[i] else src.at[:, cut((1 - me.c) * width, width)]
        send(theirs, dst.at[me.c], send_sem.at[i], recv_sem.at[i], me.sibling())
    for i, dst in enumerate(outs):
        local[i].wait()
        local[i] = pltpu.make_async_copy(staged[i], dst.at[me.c], local_sem.at[i, 1])
        local[i].start()
    for i, copy in enumerate(send.pending):
        local[i].wait()
        copy.wait_recv()
    send.drain()


def exchange(arrays, whole):
    count = len(arrays)
    outs = []
    for array, full in zip(arrays, whole):
        rows, width = array.shape
        outs.append(jax.ShapeDtypeStruct((2, rows, width if full else width // 2), array.dtype))
    results = pl.pallas_call(
        lambda *refs: exchange_kernel(whole, *refs),
        out_shape=outs,
        in_specs=[ANY] * count,
        out_specs=[ANY] * count,
        scratch_shapes=[DMA((count,))] * 2 + [DMA((count, 2))] + [pltpu.VMEM(out.shape[1:], out.dtype) for out in outs],
        compiler_params=pltpu.CompilerParams(collective_id=2, has_side_effects=True, vmem_limit_bytes=24 * 2**20),
        name="exchange_rows",
    )(*arrays)
    return [both.reshape(-1, both.shape[-1]) for both in results]


REDUCE_ROWS = (192, 192, 192, 192, 192, 512, 64)
REDUCE_COLUMNS = (768, 768, 768, 2048, 2048, 768, 256)
REDUCE_DIMS = {"A": "zyx", "B": "yxz", "C": "xzy"}
REDUCE_UNITS = [("A", 3, i * 512, 512) for i in range(4)] + [("A", 0, 0, 768)]
REDUCE_UNITS += [("B", 4, i * 512, 512) for i in range(4)] + [("B", 1, 0, 768)]
REDUCE_UNITS += [("C", 5, i * 256, 256) for i in range(3)] + [("C", 2, 0, 768), ("C", 6, 0, 256)]
ROUNDS = [(t, 5 + t, 10 + t) for t in range(5)]
GAINS = 6


def reduce_shapes(u):
    order, a, _, n = REDUCE_UNITS[u]
    r = REDUCE_ROWS[a]
    first = {"A": (2, r, n), "B": (4, r, n // 2), "C": (2, 4, r // 4, n)}[order]
    second = {"A": (r, n // 2), "B": (4, r // 4, n // 2), "C": (2, r // 4, n)}[order]
    return first, second, (r // 4, n // 2)


def add_into(total, parts):
    *lead, rows, _ = total.shape
    blocks = rows // 16

    def step(i, carry):
        where, rest = [], i // blocks
        for n in reversed(lead):
            where.insert(0, rest % n)
            rest = rest // n
        where = (*where, rcut((i % blocks) * 16, 16), slice(None))
        s = total[where].astype(jnp.float32)
        for k in range(3):
            s = s + parts[(k, *where)].astype(jnp.float32)
        total[where] = s.astype(jnp.bfloat16)
        return carry

    lax.fori_loop(0, math.prod(lead) * blocks, step, 0)


def reduce_kernel(*refs):
    nu = len(REDUCE_UNITS)
    ins, rows_in, outs, halo, totals = refs[:7], refs[7:9], refs[9:16], refs[16], refs[17:24]
    rest = refs[24:]
    kept = (rest[:nu], rest[nu : 2 * nu], rest[2 * nu : 3 * nu])
    taken = (rest[3 * nu : 4 * nu], rest[4 * nu : 5 * nu], rest[5 * nu : 6 * nu])
    send_sem, recv_sem, g_send, g_recv, s_send, s_recv, h_send, h_recv, local_sem, final_sem = rest[6 * nu :]
    me = Place()
    meet(me.peers("z") + me.peers("x") + me.peers("y") + [me.sibling(), me.step(-1), me.step(1)])
    send = Sender()
    sent, own = {}, {}

    def share(u, stage, x, yh, yl, z):
        order, a, first, n = REDUCE_UNITS[u]
        r = REDUCE_ROWS[a] // 4
        src = ins[a] if stage == 0 else kept[stage - 1][u]
        begin = first if stage == 0 else 0
        dim = REDUCE_DIMS[order][stage]
        lead = {"A": 2, "B": 2, "C": 2}[order] if stage == 0 else len(src.shape) - 2
        columns = slice(None) if stage else cut(begin, n)
        if dim == "z":
            return src.at[:, z, :, columns] if lead == 2 else src.at[z]
        if dim == "x":
            rows = rcut(x * r, r)
            if lead == 2:
                return src.at[:, :, rows, columns]
            return src.at[:, rows] if lead == 1 else src.at[rows]
        columns = cut(begin + yl * (n // 2), n // 2)
        if lead == 2:
            return src.at[yh, :, :, columns]
        return src.at[yh, :, columns]

    def issue(u, stage):
        dim = REDUCE_DIMS[REDUCE_UNITS[u][0]][stage]
        sent[u, stage] = [
            send(share(u, stage, *where), taken[stage][u].at[i], send_sem.at[u, stage, i], recv_sem.at[u, stage, i], me.at(*where))
            for i, where in enumerate(me.along(dim))
        ]
        own[u, stage] = pltpu.make_async_copy(
            share(u, stage, me.x, me.yh, me.yl, me.z), kept[stage][u], local_sem.at[u, stage]
        )
        own[u, stage].start()

    def finish(u, stage):
        own[u, stage].wait()
        for copy in sent[u, stage]:
            copy.wait_recv()
        add_into(kept[stage][u], taken[stage][u])

    def result(u, all_x, all_y):
        order, a, first, n = REDUCE_UNITS[u]
        r = REDUCE_ROWS[a] // 4
        rows = slice(None) if all_x else rcut(me.x * r, r)
        columns = cut(first, n) if all_y else cut(first + me.yl * (n // 2), n // 2)
        return totals[a].at[rows, columns]

    def spread_one(u):
        order = REDUCE_UNITS[u][0]
        dst = result(u, False, False)
        own[u, 3] = pltpu.make_async_copy(kept[2][u], dst, local_sem.at[u, 3])
        own[u, 3].start()
        to = [me.inner()] if order == "C" else me.peers("x")
        sent[u, 3] = [send(kept[2][u], dst, g_send.at[u, i], g_recv.at[u, i], one) for i, one in enumerate(to)]

    def spread_two(u):
        order = REDUCE_UNITS[u][0]
        own[u, 3].wait()
        for copy in sent[u, 3]:
            copy.wait_recv()
        ref = result(u, order != "C", order == "C")
        to = me.peers("x") if order == "C" else [me.inner()]
        sent[u, 4] = [send(ref, ref, g_send.at[u, 3 + i], g_recv.at[u, 3 + i], one) for i, one in enumerate(to)]

    last = []

    def deliver(u):
        order, a, first, n = REDUCE_UNITS[u]
        for copy in sent[u, 4]:
            copy.wait_recv()
        if a == GAINS:
            own[u, 5] = pltpu.make_async_copy(totals[a], outs[a], final_sem.at[u])
            own[u, 5].start()
            return
        r, width = REDUCE_ROWS[a] // 2, REDUCE_COLUMNS[a]
        dst = outs[a].at[:, cut(me.c * width + first, n)]
        last.append(send(totals[a].at[rcut((1 - me.c) * r, r), cut(first, n)], dst, s_send.at[u], s_recv.at[u], me.sibling()))
        own[u, 5] = pltpu.make_async_copy(totals[a].at[rcut(me.c * r, r), cut(first, n)], dst, final_sem.at[u])
        own[u, 5].start()

    for i, src in enumerate(rows_in):
        last.append(send(src.at[:, pl.ds(BIN, HALO)], halo.at[i], h_send.at[i], h_recv.at[i], me.step(1)))
    count = len(ROUNDS)
    for u in ROUNDS[0]:
        issue(u, 0)
    for t in range(count + 4):
        if t + 1 < count:
            for u in ROUNDS[t + 1]:
                issue(u, 0)
        for stage in range(2):
            if 0 <= t - stage < count:
                for u in ROUNDS[t - stage]:
                    finish(u, stage)
                    issue(u, stage + 1)
        if 0 <= t - 2 < count:
            for u in ROUNDS[t - 2]:
                finish(u, 2)
                spread_one(u)
        if 0 <= t - 3 < count:
            for u in ROUNDS[t - 3]:
                spread_two(u)
        if 0 <= t - 4 < count:
            for u in ROUNDS[t - 4]:
                deliver(u)
    for u in range(nu):
        own[u, 5].wait()
    for copy in last:
        copy.wait_recv()
    send.drain()


def reduce_grads(grads, block_rows, input_rows):
    nu = len(REDUCE_UNITS)
    first, second, third = zip(*[reduce_shapes(u) for u in range(nu)])
    low = jnp.bfloat16
    shapes = list(zip(REDUCE_ROWS, REDUCE_COLUMNS))
    outs = [jax.ShapeDtypeStruct((r // 2, 2 * n), low) for r, n in shapes[:GAINS]]
    outs.append(jax.ShapeDtypeStruct(shapes[GAINS], low))
    outs.append(jax.ShapeDtypeStruct((2, MB, HALO, D), low))
    scratch = [pltpu.VMEM(s, low) for s in shapes]
    scratch += [pltpu.VMEM(s, low) for s in (*first, *second, *third)]
    scratch += [pltpu.VMEM((3, *s), low) for s in (*first, *second, *third)]
    scratch += [DMA((nu, 3, 3))] * 2 + [DMA((nu, 6))] * 2 + [DMA((nu,))] * 2 + [DMA((2,))] * 2 + [DMA((nu, 4)), DMA((nu,))]
    results = pl.pallas_call(
        reduce_kernel,
        out_shape=outs,
        in_specs=[ANY] * 9,
        out_specs=[ANY] * len(outs),
        scratch_shapes=scratch,
        compiler_params=pltpu.CompilerParams(collective_id=3, has_side_effects=True, vmem_limit_bytes=56 * 2**20),
        name="reduce_grads",
    )(*grads, block_rows, input_rows)
    return results[:GAINS], results[GAINS], results[GAINS + 1]


def window_layout(seq_lengths, first_row):
    count = seq_lengths.shape[0]
    ids = jnp.arange(count, dtype=jnp.int32)
    earlier = ids[None, :] < ids[:, None]
    start = jnp.sum(jnp.where(earlier, seq_lengths[None, :], 0), axis=1)
    end = start + seq_lengths
    rows = first_row + jnp.arange(WIN, dtype=jnp.int32)
    which = jnp.sum((rows[:, None] >= end[None, :]).astype(jnp.int32), axis=1)
    onehot = which[:, None] == ids[None, :]
    begin = jnp.sum(jnp.where(onehot, start[None, :], 0), axis=1)
    inside = which < count
    mine = inside & (begin >= first_row) & (begin < first_row + BIN)
    return which, rows - begin, mine, inside


def dot(a, b, dims):
    return lax.dot_general(a, b, (dims, ((), ())), preferred_element_type=jnp.float32)


def nn(a, b):
    return dot(a, b, ((1,), (0,)))


def nt(a, b):
    return dot(a, b, ((1,), (1,)))


def tn(a, b):
    return dot(a, b, ((0,), (0,)))


FF_BLOCK = 512
FF_BLOCKS = FF // FF_BLOCK
CHUNK = 4 * HEAD_WIDTH
SCALE = HEAD_WIDTH ** (-0.5)


def mean_of(value):
    return jnp.mean(value, axis=-1, keepdims=True)


def swap_halves(value):
    lane = lax.broadcasted_iota(jnp.int32, value.shape, 1) % HEAD_WIDTH
    return jnp.where(
        lane < HEAD_WIDTH // 2, pltpu.roll(value, CHUNK - HEAD_WIDTH // 2, 1), pltpu.roll(value, HEAD_WIDTH // 2, 1)
    )


def split_heads(dst, chunk, value):
    for i in range(4):
        dst[4 * chunk + i, :, :HEAD_WIDTH] = value[:, HEAD_WIDTH * i : HEAD_WIDTH * (i + 1)].astype(jnp.bfloat16)


def allowed_pairs(seg_ref, segt_ref):
    row = lax.broadcasted_iota(jnp.int32, (ROWS, ROWS), 0)
    column = lax.broadcasted_iota(jnp.int32, (ROWS, ROWS), 1)
    return (seg_ref[...] == segt_ref[...]) & (column <= row)


def probabilities(q, k, allowed):
    s = jnp.where(allowed, nt(q, k) * SCALE, -1e30)
    e = jnp.exp(s - jnp.max(s, axis=-1, keepdims=True))
    return e / jnp.sum(e, axis=-1, keepdims=True)


def second_norm(x2_ref, gain_ref, a2_ref):
    x2 = x2_ref[...]
    r2 = lax.rsqrt(mean_of(x2 * x2) + eps_norm)
    a2_ref[...] = (x2 * r2 * gain_ref[...]).astype(jnp.bfloat16)


def feedforward_block(first, a2_ref, dy_ref, wg, wu, wd, hid_ref, dg_ref, du_ref, yb_ref, da2_ref):
    at = cut(first, FF_BLOCK)
    g = nn(a2_ref[...], wg)
    u = nn(a2_ref[...], wu)
    sig = jax.nn.sigmoid(g)
    sw = g * sig
    hid = (sw * u).astype(jnp.bfloat16)
    hid_ref[:, at] = hid
    dhid = nt(dy_ref[...], wd)
    dg = (dhid * u * sig * (1.0 + g * (1.0 - sig))).astype(jnp.bfloat16)
    du = (dhid * sw).astype(jnp.bfloat16)
    dg_ref[:, at] = dg
    du_ref[:, at] = du
    yb_ref[...] += nn(hid, wd)
    da2_ref[...] += nt(dg, wg) + nt(du, wu)


def feedforward_back(dy_ref, x2_ref, da2_ref, gain_ref, dat_ref, dgain_ref):
    x2, da2 = x2_ref[...], da2_ref[...]
    r2 = lax.rsqrt(mean_of(x2 * x2) + eps_norm)
    n2 = x2 * r2
    dgain_ref[1:2, :] = jnp.sum(da2 * n2, axis=0, keepdims=True)
    e2 = da2 * gain_ref[...]
    dx2 = dy_ref[...].astype(jnp.float32) + r2 * (e2 - n2 * mean_of(e2 * n2))
    da2_ref[...] = dx2
    dat_ref[...] = dx2.astype(jnp.bfloat16)


def attention_backward(
    x_ref, gain_ref, cos_ref, sin_ref, seg_ref, segt_ref, wq, wk, wv, wo, q_ref, k_ref, v_ref, dat_ref, dx2_ref, do_ref, turn_ref, dqf_ref, dkv_ref, dx_ref, dgain_ref
):
    for chunk in range(4):
        rows = wo[chunk // 2, 2 * (chunk % 2) : 2 * (chunk % 2) + 2].reshape(CHUNK, D)
        split_heads(do_ref, chunk, nt(dat_ref[...], rows))
    allowed = allowed_pairs(seg_ref, segt_ref)
    for c in range(KEY_VALUE_HEADS):
        k, v = k_ref[c], v_ref[c]
        dk = jnp.zeros((ROWS, 128), jnp.float32)
        dv = jnp.zeros((ROWS, 128), jnp.float32)
        for head in (2 * c, 2 * c + 1):
            q, do = q_ref[head], do_ref[head]
            p = probabilities(q, k, allowed)
            dp = nt(do, v)
            ds = (p * (dp - jnp.sum(p * dp, axis=-1, keepdims=True))).astype(jnp.bfloat16)
            dq = nn(ds, k) * SCALE
            turn_ref[:, HEAD_WIDTH * head : HEAD_WIDTH * (head + 1)] = dq[:, :HEAD_WIDTH]
            dk = dk + tn(ds, q)
            dv = dv + tn(p.astype(jnp.bfloat16), do)
        dkv_ref[:, KVW + HEAD_WIDTH * c : KVW + HEAD_WIDTH * (c + 1)] = dv[:, :HEAD_WIDTH].astype(jnp.bfloat16)
        turn_ref[:, QW + HEAD_WIDTH * c : QW + HEAD_WIDTH * (c + 1)] = (dk * SCALE)[:, :HEAD_WIDTH]
    cos, sin = cos_ref[...], sin_ref[...]
    for chunk in range(6):
        value = turn_ref[:, CHUNK * chunk : CHUNK * (chunk + 1)]
        value = (value * cos - swap_halves(value) * sin).astype(jnp.bfloat16)
        if chunk < 4:
            dqf_ref[:, CHUNK * chunk : CHUNK * (chunk + 1)] = value
        else:
            dkv_ref[:, CHUNK * (chunk - 4) : CHUNK * (chunk - 3)] = value
    da1 = nt(dqf_ref[...], wq[...].reshape(D, QW)) + nt(dkv_ref[:, :KVW], wk[...].reshape(D, KVW))
    da1 = da1 + nt(dkv_ref[:, KVW:], wv[...].reshape(D, KVW))
    x = x_ref[...].astype(jnp.float32)
    r1 = lax.rsqrt(mean_of(x * x) + eps_norm)
    n1 = x * r1
    dgain_ref[0:1, :] = jnp.sum(da1 * n1, axis=0, keepdims=True)
    e1 = da1 * gain_ref[...]
    dx = dx2_ref[...] + r1 * (e1 - n1 * mean_of(e1 * n1))
    dx_ref[...] = dx.astype(jnp.bfloat16)


GATHER_UNITS = [(7, 0, 256, False), (1, 0, 768, False), (2, 0, 768, False), (4, 0, 512, True), (0, 0, 768, False), (0, 768, 768, False)]
GATHER_UNITS += [(4, 2048, 512, True), (3, 0, 768, False), (3, 768, 768, False), (5, 0, 512, True)]
GATHER_UNITS += [(6, i * 256, 256, False) for i in range(6)] + [(5, 2048 + i * 512, 512, False) for i in range(4)]
AHEAD = 3
GATE_ONE, GATE_TWO, UP_X, DOWN_LAST, UP_LAST = 3, 6, 9, 15, 19


def layer_kernel(*refs):
    parts, (tokens, cotangent, cos_ref, sin_ref, seg_ref, segt_ref, mine_ref) = refs[:8], refs[8:15]
    wg_hbm, wu_hbm, wd_hbm = refs[15:18]
    block_ref, dx_ref, a1_ref, o_ref, a2_ref, hid_ref, dqf_ref, dkv_ref, dat_ref, dg_ref, du_ref, dgain_ref, dy_ref = refs[18:31]
    wq, wk, wv, wo, gains_ref, x_ref, gain1_ref, gain2_ref, wg, wu, wd, q_ref, k_ref, v_ref, do_ref, x2_ref, da2_ref, turn_ref = refs[31:49]
    z_send, z_recv, y_send, y_recv, s_send, s_recv, x_send, x_recv, h_send, h_recv, local_sem, row_sem, block_sem = refs[49:62]
    staged = refs[62:]
    outs = (wq, wk, wv, wo, wg_hbm, wu_hbm, wd_hbm, gains_ref)
    me = Place()
    units = GATHER_UNITS
    count = len(units)
    local, z_sent, y_one, y_two, x_sent, s_sent = {}, {}, {}, {}, {}, {}

    def columns(u, half=None, quarter=None):
        array, first, width, over_x = units[u]
        if over_x:
            first = first + (me.x if quarter is None else quarter) * width
        if half is None:
            return cut(first, width)
        return cut(first + half * (width // 2), width // 2)

    for u in range(count):
        local[u] = pltpu.make_async_copy(parts[units[u][0]].at[:, columns(u)], staged[u], local_sem.at[u, 0])
        local[u].start()
    rows = []
    for i, (src, dst) in enumerate(((tokens, x_ref), (cotangent, dy_ref))):
        for m in range(MB):
            rows.append(pltpu.make_async_copy(src.at[m], dst.at[pl.ds(m * WIN, BIN)], row_sem.at[i, m]))
            rows[-1].start()
    meet(me.peers("z") + me.peers("x") + [me.cross(), me.inner(), me.sibling(), me.step(-1), me.step(1)])
    send = Sender()

    def to_sibling(u, at, ref):
        s_sent[u, at] = send(ref, ref, s_send.at[u, at], s_recv.at[u, at], me.sibling())

    def z_phase(u):
        a = units[u][0]
        dst = outs[a].at[me.yh, me.z, me.c, :, columns(u)]
        local[u].wait()
        z_sent[u] = [send(staged[u], dst, z_send.at[u, i], z_recv.at[u, i], to) for i, to in enumerate(me.peers("z"))]
        local[u] = pltpu.make_async_copy(staged[u], dst, local_sem.at[u, 1])
        local[u].start()

    def y_phase(u):
        a = units[u][0]
        local[u].wait()
        for copy in z_sent[u]:
            copy.wait_recv()
        ref = outs[a].at[me.yh, :, me.c, :, columns(u, me.half)]
        y_one[u] = send(ref, ref, y_send.at[u, 0], y_recv.at[u, 0], me.cross())
        if not units[u][3]:
            to_sibling(u, 0, outs[a].at[me.yh, :, me.c, :, columns(u)])

    def forward_phase(u):
        a = units[u][0]
        y_one[u].wait_recv()
        ref = outs[a].at[1 - me.yh, :, me.c, :, columns(u, me.half)]
        y_two[u] = send(ref, ref, y_send.at[u, 1], y_recv.at[u, 1], me.inner())

    def last_phase(u):
        a = units[u][0]
        y_two[u].wait_recv()
        if units[u][3]:
            ref = outs[a].at[:, :, me.c, :, columns(u)]
            x_sent[u] = [send(ref, ref, x_send.at[u, i], x_recv.at[u, i], to) for i, to in enumerate(me.peers("x"))]
            to_sibling(u, 3, ref)
        else:
            to_sibling(u, 1, outs[a].at[1 - me.yh, :, me.c, :, columns(u)])

    def x_phase(u, i):
        x_sent[u][i].wait_recv()
        to_sibling(u, i, outs[units[u][0]].at[:, :, me.c, :, columns(u, None, (me.x + 3 - i) % 4)])

    def arrived(*which):
        for u in which:
            for at in range(4):
                if (u, at) in s_sent:
                    s_sent.pop((u, at)).wait_recv()

    cos, sin = cos_ref[...], sin_ref[...]

    def begin():
        for copy in rows:
            copy.wait()
        for copy in halo:
            copy.wait_recv()
        keep = mine_ref[...] > 0
        x_ref[...] = jnp.where(keep, x_ref[...], jnp.zeros_like(x_ref))
        dy_ref[...] = jnp.where(keep, dy_ref[...], jnp.zeros_like(dy_ref))
        arrived(0)
        for s in range(SHARDS):
            row = gains_ref[s // 8, (s // 2) % 4, s % 2, 0:1, :].astype(jnp.float32)
            gain1_ref[:, 96 * s : 96 * (s + 1)] = row[:, :96]
            gain2_ref[:, 96 * s : 96 * (s + 1)] = row[:, 128:224]
        x = x_ref[...].astype(jnp.float32)
        a1_ref[...] = (x * lax.rsqrt(mean_of(x * x) + eps_norm) * gain1_ref[...]).astype(jnp.bfloat16)
        for ref in (q_ref, k_ref, v_ref, do_ref):
            ref[:, :, HEAD_WIDTH:] = jnp.zeros((ref.shape[0], ROWS, 128 - HEAD_WIDTH), jnp.bfloat16)

    def project(weight, dst, chunk, turned):
        value = nn(a1_ref[...], weight[:, :, :, :, CHUNK * chunk : CHUNK * (chunk + 1)].reshape(D, CHUNK))
        if turned:
            value = value * cos + swap_halves(value) * sin
        split_heads(dst, chunk, value)

    def attend(first):
        allowed = allowed_pairs(seg_ref, segt_ref)
        for head in range(first, first + 4):
            p = probabilities(q_ref[head], k_ref[head // 2], allowed)
            o = nn(p.astype(jnp.bfloat16), v_ref[head // 2])
            o_ref[:, HEAD_WIDTH * head : HEAD_WIDTH * (head + 1)] = o[:, :HEAD_WIDTH].astype(jnp.bfloat16)

    def out_project(part):
        at = slice(768 * part, 768 * (part + 1))
        x2_ref[:, at] = x_ref[:, at].astype(jnp.float32) + nn(o_ref[...], wo[:, :, :, :, at].reshape(QW, 768))

    yb_ref = turn_ref.at[:, :D]

    def between():
        second_norm(x2_ref, gain2_ref, a2_ref)
        yb_ref[...] = x2_ref[...]
        da2_ref[...] = jnp.zeros_like(da2_ref)

    loads = []

    def block_load(first):
        slot = len(loads) % 2
        pair = first // FF_BLOCK
        copies = [
            pltpu.make_async_copy(wg_hbm.at[:, :, :, :, cut(first, FF_BLOCK)], wg.at[slot], block_sem.at[slot, 0]),
            pltpu.make_async_copy(wu_hbm.at[:, :, :, :, cut(first, FF_BLOCK)], wu.at[slot], block_sem.at[slot, 1]),
            pltpu.make_async_copy(wd_hbm.at[pair // 4, pair % 4], wd.at[slot], block_sem.at[slot, 2]),
        ]
        for copy in copies:
            copy.start()
        loads.append((first, slot, copies))

    done = []

    def block_compute():
        first, slot, copies = loads[len(done)]
        done.append(first)
        for copy in copies:
            copy.wait()
        feedforward_block(
            first, a2_ref, dy_ref, wg[slot].reshape(D, FF_BLOCK), wu[slot].reshape(D, FF_BLOCK), wd[slot].reshape(FF_BLOCK, D),
            hid_ref, dg_ref, du_ref, yb_ref, da2_ref,
        )

    halo = []
    for i, (src, dst) in enumerate(((tokens, x_ref), (cotangent, dy_ref))):
        for m in range(MB):
            there = dst.at[pl.ds(m * WIN + BIN, HALO)]
            halo.append(send(src.at[m, pl.ds(0, HALO)], there, h_send.at[i, m], h_recv.at[i, m], me.step(-1)))

    def quarter(i):
        return ((me.x + 3 - i) % 4) * FF_BLOCK

    def x_quarters(u):
        for i in range(3):
            x_phase(u, i)

    pieces = {
        3: [begin],
        4: [lambda: arrived(1), lambda: project(wk, k_ref, 0, True), lambda: project(wk, k_ref, 1, True)],
        5: [lambda: arrived(2), lambda: project(wv, v_ref, 0, False), lambda: project(wv, v_ref, 1, False)],
        7: [lambda: arrived(4), lambda: project(wq, q_ref, 0, True)],
        8: [lambda: project(wq, q_ref, 1, True), lambda: arrived(5)],
        9: [lambda: project(wq, q_ref, 2, True)],
        10: [lambda: project(wq, q_ref, 3, True)],
        11: [lambda: attend(0), lambda: x_quarters(GATE_ONE)],
        12: [lambda: attend(4)],
        13: [lambda: attend(8)],
        14: [lambda: attend(12)],
        15: [lambda: x_quarters(GATE_TWO), lambda: arrived(7, 8), lambda: out_project(0)],
        16: [lambda: out_project(1)],
        17: [between],
        18: [lambda: arrived(GATE_ONE, UP_X, *range(10, 16)), lambda: block_load(me.x * FF_BLOCK)],
        19: [lambda: arrived(GATE_TWO, 16), lambda: block_load(2048), block_compute],
        20: [lambda: arrived(17), lambda: x_quarters(UP_X), lambda: block_load(2048 + FF_BLOCK) , block_compute],
        21: [block_compute, lambda: arrived(18), lambda: block_load(2048 + 2 * FF_BLOCK)],
    }
    for u in range(AHEAD):
        z_phase(u)
    for t in range(count + 2):
        if t + AHEAD < count:
            z_phase(t + AHEAD)
        if t < count:
            y_phase(t)
        if 1 <= t <= count:
            forward_phase(t - 1)
        if t >= 2:
            last_phase(t - 2)
        for piece in pieces.get(t, ()):
            piece()
    arrived(UP_X)
    for i in range(3):
        block_load(quarter(i))
        block_compute()
    arrived(UP_LAST)
    block_load(2048 + 3 * FF_BLOCK)
    block_compute()
    block_compute()
    block_ref[...] = yb_ref[...].astype(jnp.bfloat16)
    dgain_ref[...] = jnp.zeros_like(dgain_ref)
    feedforward_back(dy_ref, x2_ref, da2_ref, gain2_ref, dat_ref, dgain_ref)
    attention_backward(
        x_ref, gain1_ref, cos_ref, sin_ref, seg_ref, segt_ref, wq, wk, wv, wo, q_ref, k_ref, v_ref, dat_ref, da2_ref, do_ref, turn_ref, dqf_ref, dkv_ref, dx_ref, dgain_ref
    )
    assert not s_sent and len(done) == FF_BLOCKS
    send.drain()


def layer_pass(parts, tokens, cotangent, seg, position, mine):
    low, full = jnp.bfloat16, jnp.float32
    half = HEAD_WIDTH // 2
    freq = jnp.exp(jnp.arange(half, dtype=full) * (-2.0 * math.log(rope_base) / HEAD_WIDTH))
    angle = position.astype(full)[:, None] * freq[None, :]
    cos, sin = jnp.cos(angle), jnp.sin(angle)
    cos = jnp.tile(cos, (1, 8))
    sin = jnp.tile(jnp.concatenate([-sin, sin], axis=1), (1, 4))
    count = len(GATHER_UNITS)
    outs = [jax.ShapeDtypeStruct((2, 4, 2, *parts[a].shape), low) for a in (4, 5, 6)]
    wide = [(D, low), (D, low), (D, low), (QW, low), (D, low), (FF, low), (QW, low), (2 * KVW, low), (D, low), (FF, low), (FF, low)]
    outs += [jax.ShapeDtypeStruct((ROWS, n), t) for n, t in wide] + [jax.ShapeDtypeStruct((8, D), full)]
    outs += [jax.ShapeDtypeStruct((ROWS, D), low)]
    vmem = pl.BlockSpec(memory_space=pltpu.VMEM)
    scratch = [pltpu.VMEM((2, 4, 2, *parts[a].shape), low) for a in (0, 1, 2, 3, 7)]
    scratch += [pltpu.VMEM((ROWS, D), low), pltpu.VMEM((1, D), full), pltpu.VMEM((1, D), full)]
    scratch += [pltpu.VMEM((2, 2, 4, 2, 96, FF_BLOCK), low)] * 2 + [pltpu.VMEM((2, 2, 256, D), low)]
    scratch += [pltpu.VMEM((n, ROWS, 128), low) for n in (QUERY_HEADS, KEY_VALUE_HEADS, KEY_VALUE_HEADS, QUERY_HEADS)]
    scratch += [pltpu.VMEM((ROWS, D), full), pltpu.VMEM((ROWS, D), full), pltpu.VMEM((ROWS, QW + KVW), full)]
    scratch += [DMA((count, 3))] * 2 + [DMA((count, 2))] * 2 + [DMA((count, 4))] * 2 + [DMA((count, 3))] * 2
    scratch += [DMA((2, MB))] * 2 + [DMA((count, 2)), DMA((2, MB)), DMA((2, 3))]
    scratch += [pltpu.VMEM((parts[a].shape[0], n), low) for a, _, n, _ in GATHER_UNITS]
    results = pl.pallas_call(
        layer_kernel,
        out_shape=outs,
        in_specs=[ANY] * 10 + [vmem] * 5,
        out_specs=[ANY] * 3 + [vmem] * 13,
        scratch_shapes=scratch,
        compiler_params=pltpu.CompilerParams(collective_id=1, has_side_effects=True, vmem_limit_bytes=60 * 2**20),
        name="layer",
    )(*parts, tokens, cotangent, cos, sin, seg.reshape(ROWS, 1), seg.reshape(1, ROWS), mine.astype(jnp.int32).reshape(ROWS, 1))
    return results[3:]


def body(
    tokens,
    query_weight,
    key_weight,
    value_weight,
    out_weight,
    gate_weight,
    up_weight,
    down_weight,
    attention_gain,
    feedforward_gain,
    lengths,
    deal,
    block_cotangent,
):
    me = lax.axis_index("shard")
    core = me % 2
    gains = jnp.pad(jnp.stack([attention_gain, feedforward_gain]), ((0, 0), (0, 32))).reshape(1, 256)
    gains = jnp.pad(gains, ((0, 15), (0, 0)))
    parts = (
        query_weight,
        key_weight,
        value_weight,
        out_weight,
        gate_weight,
        up_weight,
        down_weight,
        gains,
    )
    layout = [window_layout(lengths[m, 0], me * BIN) for m in range(MB)]
    seg = jnp.concatenate([one[0] + m * 64 for m, one in enumerate(layout)])
    position = jnp.concatenate([one[1] for one in layout])
    mine = jnp.concatenate([one[2] for one in layout])
    position = jnp.where(mine, position, 0)
    block_rows, input_rows, a1, o, a2, hid, dqf, dkv, dat, dg, du, dgain, dy = layer_pass(
        parts, tokens, block_cotangent, seg, position, mine
    )

    gain_rows = jnp.pad(dgain.astype(jnp.bfloat16), ((0, 8), (0, 0)))
    arrays = (a1, o, a2, hid, gain_rows, dqf, dkv, dat, dg, du, dy)
    both = exchange(arrays, (True,) * 5 + (False,) * 6)
    a1, o, a2, hid, gain_both, dqf, dkv, dat, dg, du, dy = both
    pairs = ((a1, dqf), (a1, dkv), (o, dat), (a2, dg), (a2, du), (hid, dy))
    grads = [tn(left, right).astype(jnp.bfloat16) for left, right in pairs]
    grads = [grad.reshape(2, 4, -1, grad.shape[-1]) for grad in grads]
    gain_both = gain_both.astype(jnp.float32).reshape(2, 16, D)
    gain_sum = (gain_both[0, :2] + gain_both[1, :2]).reshape(2, 2, 4, 192).transpose(1, 2, 0, 3)
    gain_sum = jnp.pad(gain_sum, ((0, 0), (0, 0), (0, 62), (0, 64))).astype(jnp.bfloat16)
    totals, gain_totals, from_before = reduce_grads(
        (*grads, gain_sum), block_rows.reshape(MB, WIN, D), input_rows.reshape(MB, WIN, D)
    )

    results = jnp.stack([block_rows, input_rows]).reshape(2, MB, WIN, D)[:, :, :BIN]
    from_before = jnp.pad(from_before, ((0, 0), (0, 0), (0, BIN - HALO), (0, 0)))
    mine_own = jnp.stack([one[2][:BIN] for one in layout])[None, :, :, None]
    inside = jnp.stack([one[3][:BIN] for one in layout])[None, :, :, None]
    rows_out = jnp.where(mine_own, results, jnp.where(inside, from_before, 0))
    g_query, g_kv, g_out, g_gate, g_up, g_down = [total.astype(jnp.float32) for total in totals]
    gain_out = lax.dynamic_slice_in_dim(gain_totals[:2].astype(jnp.float32), core * 96, 96, axis=1)
    return (
        rows_out[0],
        rows_out[1],
        g_query,
        g_kv[:, :KVW],
        g_kv[:, KVW:],
        g_out,
        g_gate,
        g_up,
        g_down,
        gain_out[0],
        gain_out[1],
    )


def solution(mesh):
    placed = (
        P(None, ("rep", "shard"), None),
        *([P("shard", None)] * 7),
        P("shard"),
        P("shard"),
        P(None, "rep", None),
        P(None, "rep", None),
        P(None, ("rep", "shard"), None),
    )
    return jax.shard_map(
        body,
        mesh=mesh,
        in_specs=placed,
        out_specs=(
            P(None, ("rep", "shard"), None),
            P(None, ("rep", "shard"), None),
            *([P("shard", None)] * 7),
            P("shard"),
            P("shard"),
        ),
        check_vma=False,
    )
```

```python
import math

import jax
import jax.numpy as jnp
from jax import lax
from jax.experimental import pallas as pl
from jax.experimental.pallas import tpu as pltpu
from jax.sharding import PartitionSpec as P

D = 1536
QUERY_HEADS = 16
KEY_VALUE_HEADS = 8
HEAD_WIDTH = 96
QW = QUERY_HEADS * HEAD_WIDTH
KVW = KEY_VALUE_HEADS * HEAD_WIDTH
FF = 4096
BIN = 64
HALO = 48
WIN = BIN + HALO
MB = 2
SHARDS = 16
ROWS = MB * WIN
MESH = pl.DeviceIdType.MESH
ANY = pl.BlockSpec(memory_space=pl.ANY)
DMA = pltpu.SemaphoreType.DMA

eps_norm = 1e-05
rope_base = 100000.0


class Place:
    def __init__(self):
        rep, shard = lax.axis_index("rep"), lax.axis_index("shard")
        self.rep, self.shard = rep, shard
        self.x, self.yl = rep // 2, rep % 2
        self.yh, self.z, self.c = shard // 8, (shard // 2) % 4, shard % 2
        self.y = self.yh * 2 + self.yl
        self.half = jnp.where(self.yh == self.yl, 1, 0)

    def at(self, x=None, yh=None, yl=None, z=None, c=None):
        def pick(new, old):
            return old if new is None else new

        rep = pick(x, self.x) * 2 + pick(yl, self.yl)
        return rep, pick(yh, self.yh) * 8 + pick(z, self.z) * 2 + pick(c, self.c)

    def along(self, dim):
        found = []
        for o in (1, 2, 3):
            x, yh, yl, z = self.x, self.yh, self.yl, self.z
            if dim == "x":
                x = (x + o) % 4
            elif dim == "z":
                z = (z + o) % 4
            else:
                y = (self.y + o) % 4
                yh, yl = y // 2, y % 2
            found.append((x, yh, yl, z))
        return found

    def peers(self, dim):
        return [self.at(*where) for where in self.along(dim)]

    def cross(self):
        return self.at(yh=1 - self.yh, yl=1 - self.yl)

    def inner(self):
        return self.at(yl=1 - self.yl)

    def sibling(self):
        return self.at(c=1 - self.c)

    def step(self, by):
        return self.rep, (self.shard + by + SHARDS) % SHARDS


def meet(peers):
    barrier = pltpu.get_barrier_semaphore()
    for peer in peers:
        pl.semaphore_signal(barrier, inc=1, device_id=peer, device_id_type=MESH)
    pl.semaphore_wait(barrier, len(peers))


class Sender:
    def __init__(self):
        self.pending = []

    def __call__(self, src, dst, send_sem, recv_sem, to):
        copy = pltpu.make_async_remote_copy(
            src_ref=src,
            dst_ref=dst,
            send_sem=send_sem,
            recv_sem=recv_sem,
            device_id=to,
            device_id_type=MESH,
        )
        copy.start()
        self.pending.append(copy)
        return copy

    def drain(self):
        for copy in self.pending:
            copy.wait_send()


def cut(first, count):
    if isinstance(first, int):
        return pl.ds(first, count)
    return pl.ds(pl.multiple_of(first, 128), count)


def rcut(first, count):
    if isinstance(first, int):
        return pl.ds(first, count)
    return pl.ds(pl.multiple_of(first, 16), count)


REDUCE_ROWS = (192, 192, 192, 192, 192, 512, 64)
REDUCE_COLUMNS = (768, 768, 768, 2048, 2048, 768, 256)
REDUCE_DIMS = {"A": "zyx", "B": "yxz", "C": "xzy"}
REDUCE_UNITS = [("A", 3, i * 512, 512) for i in range(4)] + [("A", 0, i * 256, 256) for i in range(3)]
REDUCE_UNITS += [("B", 4, i * 512, 512) for i in range(4)] + [("B", 1, i * 256, 256) for i in range(3)]
REDUCE_UNITS += [("C", 5, i * 256, 256) for i in range(3)] + [("C", 6, 0, 256)] + [("C", 2, i * 256, 256) for i in range(3)]
ROUNDS = [(t, 7 + t, 14 + t) for t in range(7)]
HELD = {"A": (2, 192, 512), "B": (4, 192, 256), "C": (2, 4, 128, 256)}
GAINS = 6


def reduce_shapes(u):
    order, a, _, n = REDUCE_UNITS[u]
    r = REDUCE_ROWS[a]
    first = {"A": (2, r, n), "B": (4, r, n // 2), "C": (2, 4, r // 4, n)}[order]
    second = {"A": (r, n // 2), "B": (4, r // 4, n // 2), "C": (2, r // 4, n)}[order]
    return first, second, (r // 4, n // 2)


def add_into(total, parts):
    *lead, rows, _ = total.shape
    blocks = rows // 16

    def step(i, carry):
        where, rest = [], i // blocks
        for n in reversed(lead):
            where.insert(0, rest % n)
            rest = rest // n
        where = (*where, rcut((i % blocks) * 16, 16), slice(None))
        s = total[where].astype(jnp.float32)
        for part in parts:
            s = s + part[where].astype(jnp.float32)
        total[where] = s.astype(jnp.bfloat16)
        return carry

    lax.fori_loop(0, math.prod(lead) * blocks, step, 0)


def side(ref, which):
    count = ref.shape[0] // 2
    return ref.at[pl.ds(which * count, count)]


LEFT_OF = (0, 0, 1, 2, 2, 3)
LEFTS, RIGHTS = 4, 6


def reduce_kernel(*refs):
    nu = len(REDUCE_UNITS)
    lefts_hbm, rights_hbm, dgain_hbm, rows_in = refs[:4], refs[4:10], refs[10], refs[11:13]
    outs, halo, ins, totals = refs[13:20], refs[20], refs[21:28], refs[28:35]
    rest = refs[35:]
    kept = (rest[:nu], rest[nu : 2 * nu], rest[2 * nu : 3 * nu])
    taken = (rest[3 * nu : 4 * nu], rest[4 * nu : 5 * nu], rest[5 * nu : 6 * nu])
    rest = rest[6 * nu :]
    own_rows, their_rows, tiles, held = rest[:11], rest[11:22], rest[22:25], (rest[25:28], rest[28:31])
    send_sem, recv_sem, g_send, g_recv, s_send, s_recv, h_send, h_recv, local_sem, final_sem, e_send, e_recv, e_local, tile_sem, ring_send, ring_recv, held_sem = rest[31:]
    me = Place()
    wanted = (7, 2, 3, 6, 8, 9, 0, 1, 4, 5, 10)
    own_copies, their_copies = {}, {}
    sources = (*lefts_hbm, *rights_hbm, dgain_hbm)

    def part(i, core):
        width = own_rows[i].shape[-1]
        return sources[i].at[:, cut(core * width, width)] if LEFTS <= i < LEFTS + RIGHTS else sources[i]

    for i in wanted:
        own_copies[i] = pltpu.make_async_copy(part(i, me.c), own_rows[i], e_local.at[i])
        own_copies[i].start()
    meet(me.peers("z") + me.peers("x") + me.peers("y") + [me.sibling(), me.step(-1), me.step(1)])
    send = Sender()
    sent, own = {}, {}
    for i in wanted:
        their_copies[i] = send(part(i, 1 - me.c), their_rows[i], e_send.at[i], e_recv.at[i], me.sibling())

    def here(*which):
        for i in which:
            if i in own_copies:
                own_copies.pop(i).wait()
                their_copies.pop(i).wait_recv()

    stored = {}

    def slot_of(u):
        order, a, _, n = REDUCE_UNITS[u]
        return "ABC".index(order)

    def product(u):
        order, a, first, n = REDUCE_UNITS[u]
        slot = slot_of(u)
        flush(slot)
        r = REDUCE_ROWS[a]
        view = tiles[slot].at[:, :, :r, :n]
        if a == GAINS:
            here(10)
            view[...] = jnp.zeros((2, 4, r, n), jnp.bfloat16)
            both = own_rows[10][...] + their_rows[10][...]
            both = jnp.concatenate([both, jnp.zeros_like(both)], axis=0)
            for k in range(8):
                tiles[slot][k // 4, k % 4, :16, :192] = both[:, 192 * k : 192 * (k + 1)].astype(jnp.bfloat16)
        else:
            left, right = LEFT_OF[a], LEFTS + a
            here(left, right)
            for k in range(4):
                rows, columns = slice(2 * r * k, 2 * r * (k + 1)), slice(first, first + n)
                value = tn(own_rows[left][:, rows], own_rows[right][:, columns])
                value = value + tn(their_rows[left][:, rows], their_rows[right][:, columns])
                view[k // 2, 2 * (k % 2) : 2 * (k % 2) + 2] = value.astype(jnp.bfloat16).reshape(2, r, n)
        copy = pltpu.make_async_copy(view, ins[a].at[:, :, :, cut(first, n)], tile_sem.at[slot])
        copy.start()
        stored[slot] = copy, u

    def flush(slot):
        if slot in stored:
            copy, u = stored.pop(slot)
            copy.wait()
            issue_first(u)

    def share(u, stage, x, yh, yl, z):
        order, a, first, n = REDUCE_UNITS[u]
        r = REDUCE_ROWS[a] // 4
        src = ins[a] if stage == 0 else kept[stage - 1][u]
        begin = first if stage == 0 else 0
        dim = REDUCE_DIMS[order][stage]
        lead = {"A": 2, "B": 2, "C": 2}[order] if stage == 0 else len(src.shape) - 2
        columns = slice(None) if stage else cut(begin, n)
        if dim == "z":
            return src.at[:, z, :, columns] if lead == 2 else src.at[z]
        if dim == "x":
            rows = rcut(x * r, r)
            if lead == 2:
                return src.at[:, :, rows, columns]
            return src.at[:, rows] if lead == 1 else src.at[rows]
        columns = cut(begin + yl * (n // 2), n // 2)
        if lead == 2:
            return src.at[yh, :, :, columns]
        return src.at[yh, :, columns]

    ring, holding = {}, {}

    def hold(u):
        order, a, _, n = REDUCE_UNITS[u]
        ref = held[u % 7 % 2]["ABC".index(order)]
        shape = reduce_shapes(u)[0]
        return ref.at[(*[slice(None)] * (len(shape) - 2), pl.ds(0, shape[-2]), pl.ds(0, shape[-1]))]

    def issue_first(u):
        right, opposite, left = me.along(REDUCE_DIMS[REDUCE_UNITS[u][0]][0])
        parts = [share(u, 0, *where) for where in (right, opposite, left)]
        right, left = me.at(*right), me.at(*left)
        from_left, from_right, passing = [taken[0][u].at[i] for i in range(3)]

        def go(k, src, dst, to):
            return send(src, dst, ring_send.at[u, k], ring_recv.at[u, k], to)

        ring[u] = [
            go(0, side(parts[1], 0), side(passing, 0), right),
            go(1, side(parts[1], 1), side(passing, 1), left),
            go(2, side(parts[0], 1), side(from_left, 1), right),
            go(3, side(parts[2], 0), side(from_right, 0), left),
        ]
        holding[u] = [
            pltpu.make_async_copy(side(parts[0], 0), side(hold(u), 0), held_sem.at[u, 0]),
            pltpu.make_async_copy(side(parts[2], 1), side(hold(u), 1), held_sem.at[u, 1]),
        ]
        own[u, 0] = pltpu.make_async_copy(share(u, 0, me.x, me.yh, me.yl, me.z), kept[0][u], local_sem.at[u, 0])
        for copy in (*holding[u], own[u, 0]):
            copy.start()

    def relay(u):
        right, _, left = me.along(REDUCE_DIMS[REDUCE_UNITS[u][0]][0])
        from_left, from_right, passing = [taken[0][u].at[i] for i in range(3)]
        for k, dst, to in ((0, from_left, right), (1, from_right, left)):
            holding[u][k].wait()
            ring[u][k].wait_recv()
            add_into(side(passing, k), [side(hold(u), k)])
            ring[u].append(send(side(passing, k), side(dst, k), ring_send.at[u, 4 + k], ring_recv.at[u, 4 + k], me.at(*to)))

    def finish_first(u):
        own[u, 0].wait()
        for copy in ring[u][2:]:
            copy.wait_recv()
        add_into(kept[0][u], [taken[0][u].at[0], taken[0][u].at[1]])

    def issue(u, stage):
        dim = REDUCE_DIMS[REDUCE_UNITS[u][0]][stage]
        sent[u, stage] = [
            send(share(u, stage, *where), taken[stage][u].at[i], send_sem.at[u, stage, i], recv_sem.at[u, stage, i], me.at(*where))
            for i, where in enumerate(me.along(dim))
        ]
        own[u, stage] = pltpu.make_async_copy(
            share(u, stage, me.x, me.yh, me.yl, me.z), kept[stage][u], local_sem.at[u, stage]
        )
        own[u, stage].start()

    def finish(u, stage):
        own[u, stage].wait()
        for copy in sent[u, stage]:
            copy.wait_recv()
        add_into(kept[stage][u], [taken[stage][u].at[i] for i in range(3)])

    def result(u, all_x, all_y):
        order, a, first, n = REDUCE_UNITS[u]
        r = REDUCE_ROWS[a] // 4
        rows = slice(None) if all_x else rcut(me.x * r, r)
        columns = cut(first, n) if all_y else cut(first + me.yl * (n // 2), n // 2)
        return totals[a].at[rows, columns]

    def spread_one(u):
        order = REDUCE_UNITS[u][0]
        dst = result(u, False, False)
        own[u, 3] = pltpu.make_async_copy(kept[2][u], dst, local_sem.at[u, 3])
        own[u, 3].start()
        to = [me.inner()] if order == "C" else me.peers("x")
        sent[u, 3] = [send(kept[2][u], dst, g_send.at[u, i], g_recv.at[u, i], one) for i, one in enumerate(to)]

    def spread_two(u):
        order = REDUCE_UNITS[u][0]
        own[u, 3].wait()
        for copy in sent[u, 3]:
            copy.wait_recv()
        ref = result(u, order != "C", order == "C")
        to = me.peers("x") if order == "C" else [me.inner()]
        sent[u, 4] = [send(ref, ref, g_send.at[u, 3 + i], g_recv.at[u, 3 + i], one) for i, one in enumerate(to)]

    last = []

    def deliver(u):
        order, a, first, n = REDUCE_UNITS[u]
        for copy in sent[u, 4]:
            copy.wait_recv()
        if a == GAINS:
            own[u, 5] = pltpu.make_async_copy(totals[a], outs[a], final_sem.at[u])
            own[u, 5].start()
            return
        r, width = REDUCE_ROWS[a] // 2, REDUCE_COLUMNS[a]
        dst = outs[a].at[:, cut(me.c * width + first, n)]
        last.append(send(totals[a].at[rcut((1 - me.c) * r, r), cut(first, n)], dst, s_send.at[u], s_recv.at[u], me.sibling()))
        own[u, 5] = pltpu.make_async_copy(totals[a].at[rcut(me.c * r, r), cut(first, n)], dst, final_sem.at[u])
        own[u, 5].start()

    for i, src in enumerate(rows_in):
        last.append(send(src.at[:, pl.ds(BIN, HALO)], halo.at[i], h_send.at[i], h_recv.at[i], me.step(1)))
    count = len(ROUNDS)

    def produce(t):
        for u in ROUNDS[t]:
            product(u)
            for slot in sorted(stored):
                if slot != slot_of(u):
                    flush(slot)
        for slot in sorted(stored):
            flush(slot)

    produce(0)
    steps = (
        (0, relay),
        (1, lambda u: (finish_first(u), issue(u, 1))),
        (2, lambda u: (finish(u, 1), issue(u, 2))),
        (3, lambda u: (finish(u, 2), spread_one(u))),
        (4, spread_two),
        (5, deliver),
    )
    for t in range(count + 5):
        if t + 1 < count:
            produce(t + 1)
        for late, step in steps:
            if 0 <= t - late < count:
                for u in ROUNDS[t - late]:
                    step(u)
    for u in range(nu):
        own[u, 5].wait()
    for copy in last:
        copy.wait_recv()
    send.drain()


def reduce_grads(lefts, rights, dgain, block_rows, input_rows):
    nu = len(REDUCE_UNITS)
    first, second, third = zip(*[reduce_shapes(u) for u in range(nu)])
    low = jnp.bfloat16
    shapes = list(zip(REDUCE_ROWS, REDUCE_COLUMNS))
    outs = [jax.ShapeDtypeStruct((r // 2, 2 * n), low) for r, n in shapes[:GAINS]]
    outs.append(jax.ShapeDtypeStruct(shapes[GAINS], low))
    outs.append(jax.ShapeDtypeStruct((2, MB, HALO, D), low))
    outs += [jax.ShapeDtypeStruct((2, 4, r, n), low) for r, n in shapes]
    scratch = [pltpu.VMEM(s, low) for s in shapes]
    scratch += [pltpu.VMEM(s, low) for s in (*first, *second, *third)]
    scratch += [pltpu.VMEM((3, *s), low) for s in (*first, *second, *third)]
    rows = [pltpu.VMEM(left.shape, low) for left in lefts]
    rows += [pltpu.VMEM((ROWS, right.shape[1] // 2), low) for right in rights] + [pltpu.VMEM((8, D), jnp.float32)]
    scratch += rows * 2 + [pltpu.VMEM((2, 4, 192, 512), low)] * 2 + [pltpu.VMEM((2, 4, 512, 256), low)]
    scratch += [pltpu.VMEM(HELD[order], low) for order in "ABC"] * 2
    scratch += [DMA((nu, 3, 3))] * 2 + [DMA((nu, 6))] * 2 + [DMA((nu,))] * 2 + [DMA((2,))] * 2 + [DMA((nu, 4)), DMA((nu,))]
    scratch += [DMA((11,))] * 3 + [DMA((3,))] + [DMA((nu, 6))] * 2 + [DMA((nu, 2))]
    results = pl.pallas_call(
        reduce_kernel,
        out_shape=outs,
        in_specs=[ANY] * 13,
        out_specs=[ANY] * len(outs),
        scratch_shapes=scratch,
        compiler_params=pltpu.CompilerParams(collective_id=3, has_side_effects=True, vmem_limit_bytes=60 * 2**20),
        name="reduce_grads",
    )(*lefts, *rights, dgain, block_rows, input_rows)
    return results[:GAINS], results[GAINS], results[GAINS + 1]


def window_layout(seq_lengths, first_row):
    count = seq_lengths.shape[0]
    ids = jnp.arange(count, dtype=jnp.int32)
    earlier = ids[None, :] < ids[:, None]
    start = jnp.sum(jnp.where(earlier, seq_lengths[None, :], 0), axis=1)
    end = start + seq_lengths
    rows = first_row + jnp.arange(WIN, dtype=jnp.int32)
    which = jnp.sum((rows[:, None] >= end[None, :]).astype(jnp.int32), axis=1)
    onehot = which[:, None] == ids[None, :]
    begin = jnp.sum(jnp.where(onehot, start[None, :], 0), axis=1)
    inside = which < count
    mine = inside & (begin >= first_row) & (begin < first_row + BIN)
    return which, rows - begin, mine, inside


def dot(a, b, dims):
    return lax.dot_general(a, b, (dims, ((), ())), preferred_element_type=jnp.float32)


def nn(a, b):
    return dot(a, b, ((1,), (0,)))


def nt(a, b):
    return dot(a, b, ((1,), (1,)))


def tn(a, b):
    return dot(a, b, ((0,), (0,)))


FF_BLOCK = 512
FF_BLOCKS = FF // FF_BLOCK
CHUNK = 4 * HEAD_WIDTH
SCALE = HEAD_WIDTH ** (-0.5)


def mean_of(value):
    return jnp.mean(value, axis=-1, keepdims=True)


def swap_halves(value):
    lane = lax.broadcasted_iota(jnp.int32, value.shape, 1) % HEAD_WIDTH
    return jnp.where(
        lane < HEAD_WIDTH // 2, pltpu.roll(value, CHUNK - HEAD_WIDTH // 2, 1), pltpu.roll(value, HEAD_WIDTH // 2, 1)
    )


def split_heads(dst, chunk, value):
    for i in range(4):
        dst[4 * chunk + i, :, :HEAD_WIDTH] = value[:, HEAD_WIDTH * i : HEAD_WIDTH * (i + 1)].astype(jnp.bfloat16)


def allowed_pairs(seg_ref, segt_ref):
    row = lax.broadcasted_iota(jnp.int32, (ROWS, ROWS), 0)
    column = lax.broadcasted_iota(jnp.int32, (ROWS, ROWS), 1)
    return (seg_ref[...] == segt_ref[...]) & (column <= row)


def probabilities(q, k, allowed):
    s = jnp.where(allowed, nt(q, k) * SCALE, -1e30)
    e = jnp.exp(s - jnp.max(s, axis=-1, keepdims=True))
    return e / jnp.sum(e, axis=-1, keepdims=True)


def second_norm(x2_ref, gain_ref, a2_ref):
    x2 = x2_ref[...]
    r2 = lax.rsqrt(mean_of(x2 * x2) + eps_norm)
    a2_ref[...] = (x2 * r2 * gain_ref[...]).astype(jnp.bfloat16)


def feedforward_block(first, a2_ref, dy_ref, wg, wu, wd, hid_ref, dg_ref, du_ref, yb_ref, da2_ref):
    at = cut(first, FF_BLOCK)
    g = nn(a2_ref[...], wg)
    u = nn(a2_ref[...], wu)
    sig = jax.nn.sigmoid(g)
    sw = g * sig
    hid = (sw * u).astype(jnp.bfloat16)
    hid_ref[:, at] = hid
    dhid = nt(dy_ref[...], wd)
    dg = (dhid * u * sig * (1.0 + g * (1.0 - sig))).astype(jnp.bfloat16)
    du = (dhid * sw).astype(jnp.bfloat16)
    dg_ref[:, at] = dg
    du_ref[:, at] = du
    yb_ref[...] += nn(hid, wd)
    da2_ref[...] += nt(dg, wg) + nt(du, wu)


def feedforward_back(dy_ref, x2_ref, da2_ref, gain_ref, dat_ref, dgain_ref):
    x2, da2 = x2_ref[...], da2_ref[...]
    r2 = lax.rsqrt(mean_of(x2 * x2) + eps_norm)
    n2 = x2 * r2
    dgain_ref[1:2, :] = jnp.sum(da2 * n2, axis=0, keepdims=True)
    e2 = da2 * gain_ref[...]
    dx2 = dy_ref[...].astype(jnp.float32) + r2 * (e2 - n2 * mean_of(e2 * n2))
    da2_ref[...] = dx2
    dat_ref[...] = dx2.astype(jnp.bfloat16)


def attention_backward(
    x_ref, gain_ref, cos_ref, sin_ref, seg_ref, segt_ref, wq, wk, wv, wo, q_ref, k_ref, v_ref, dat_ref, dx2_ref, do_ref, turn_ref, dqf_ref, dkv_ref, dx_ref, dgain_ref
):
    for chunk in range(4):
        rows = wo[chunk // 2, 2 * (chunk % 2) : 2 * (chunk % 2) + 2].reshape(CHUNK, D)
        split_heads(do_ref, chunk, nt(dat_ref[...], rows))
    allowed = allowed_pairs(seg_ref, segt_ref)
    for c in range(KEY_VALUE_HEADS):
        k, v = k_ref[c], v_ref[c]
        dk = jnp.zeros((ROWS, 128), jnp.float32)
        dv = jnp.zeros((ROWS, 128), jnp.float32)
        for head in (2 * c, 2 * c + 1):
            q, do = q_ref[head], do_ref[head]
            p = probabilities(q, k, allowed)
            dp = nt(do, v)
            ds = (p * (dp - jnp.sum(p * dp, axis=-1, keepdims=True))).astype(jnp.bfloat16)
            dq = nn(ds, k) * SCALE
            turn_ref[:, HEAD_WIDTH * head : HEAD_WIDTH * (head + 1)] = dq[:, :HEAD_WIDTH]
            dk = dk + tn(ds, q)
            dv = dv + tn(p.astype(jnp.bfloat16), do)
        dkv_ref[:, KVW + HEAD_WIDTH * c : KVW + HEAD_WIDTH * (c + 1)] = dv[:, :HEAD_WIDTH].astype(jnp.bfloat16)
        turn_ref[:, QW + HEAD_WIDTH * c : QW + HEAD_WIDTH * (c + 1)] = (dk * SCALE)[:, :HEAD_WIDTH]
    cos, sin = cos_ref[...], sin_ref[...]
    for chunk in range(6):
        value = turn_ref[:, CHUNK * chunk : CHUNK * (chunk + 1)]
        value = (value * cos - swap_halves(value) * sin).astype(jnp.bfloat16)
        if chunk < 4:
            dqf_ref[:, CHUNK * chunk : CHUNK * (chunk + 1)] = value
        else:
            dkv_ref[:, CHUNK * (chunk - 4) : CHUNK * (chunk - 3)] = value
    da1 = nt(dqf_ref[...], wq[...].reshape(D, QW)) + nt(dkv_ref[:, :KVW], wk[...].reshape(D, KVW))
    da1 = da1 + nt(dkv_ref[:, KVW:], wv[...].reshape(D, KVW))
    x = x_ref[...].astype(jnp.float32)
    r1 = lax.rsqrt(mean_of(x * x) + eps_norm)
    n1 = x * r1
    dgain_ref[0:1, :] = jnp.sum(da1 * n1, axis=0, keepdims=True)
    e1 = da1 * gain_ref[...]
    dx = dx2_ref[...] + r1 * (e1 - n1 * mean_of(e1 * n1))
    dx_ref[...] = dx.astype(jnp.bfloat16)


GATHER_UNITS = [(7, 0, 256, False), (1, 0, 768, False), (2, 0, 768, False), (4, 0, 512, True), (0, 0, 768, False), (0, 768, 768, False)]
GATHER_UNITS += [(4, 2048, 512, True), (3, 0, 768, False), (3, 768, 768, False), (5, 0, 512, True)]
GATHER_UNITS += [(6, i * 256, 256, False) for i in range(6)] + [(5, 2048 + i * 512, 512, False) for i in range(4)]
AHEAD = 3
GATE_ONE, GATE_TWO, UP_X, DOWN_LAST, UP_LAST = 3, 6, 9, 15, 19


def layer_kernel(*refs):
    parts, (tokens, cotangent, cos_ref, sin_ref, seg_ref, segt_ref, mine_ref) = refs[:8], refs[8:15]
    wg_hbm, wu_hbm, wd_hbm = refs[15:18]
    results = refs[18:31]
    wq, wk, wv, wo, gains_ref, x_ref, gain1_ref, gain2_ref, wg, wu, wd, q_ref, k_ref, v_ref, do_ref, x2_ref, da2_ref, turn_ref = refs[31:49]
    rows_out = refs[49:62]
    block_ref, dx_ref, a1_ref, o_ref, a2_ref, hid_ref, dqf_ref, dkv_ref, dat_ref, dg_ref, du_ref, dgain_ref, dy_ref = rows_out
    z_send, z_recv, y_send, y_recv, s_send, s_recv, x_send, x_recv, h_send, h_recv, local_sem, row_sem, block_sem, result_sem = refs[62:76]
    staged = refs[76:]
    outs = (wq, wk, wv, wo, wg_hbm, wu_hbm, wd_hbm, gains_ref)
    me = Place()
    units = GATHER_UNITS
    count = len(units)
    local, z_sent, y_one, y_two, x_sent, s_sent = {}, {}, {}, {}, {}, {}

    def columns(u, half=None, quarter=None):
        array, first, width, over_x = units[u]
        if over_x:
            first = first + (me.x if quarter is None else quarter) * width
        if half is None:
            return cut(first, width)
        return cut(first + half * (width // 2), width // 2)

    for u in range(count):
        local[u] = pltpu.make_async_copy(parts[units[u][0]].at[:, columns(u)], staged[u], local_sem.at[u, 0])
        local[u].start()
    rows = []
    for i, (src, dst) in enumerate(((tokens, x_ref), (cotangent, dy_ref))):
        for m in range(MB):
            rows.append(pltpu.make_async_copy(src.at[m], dst.at[pl.ds(m * WIN, BIN)], row_sem.at[i, m]))
            rows[-1].start()
    meet(me.peers("z") + me.peers("x") + [me.cross(), me.inner(), me.sibling(), me.step(-1), me.step(1)])
    send = Sender()

    def to_sibling(u, at, ref):
        s_sent[u, at] = send(ref, ref, s_send.at[u, at], s_recv.at[u, at], me.sibling())

    def z_phase(u):
        a = units[u][0]
        dst = outs[a].at[me.yh, me.z, me.c, :, columns(u)]
        local[u].wait()
        z_sent[u] = [send(staged[u], dst, z_send.at[u, i], z_recv.at[u, i], to) for i, to in enumerate(me.peers("z"))]
        local[u] = pltpu.make_async_copy(staged[u], dst, local_sem.at[u, 1])
        local[u].start()

    def y_phase(u):
        a = units[u][0]
        local[u].wait()
        for copy in z_sent[u]:
            copy.wait_recv()
        ref = outs[a].at[me.yh, :, me.c, :, columns(u, me.half)]
        y_one[u] = send(ref, ref, y_send.at[u, 0], y_recv.at[u, 0], me.cross())
        if not units[u][3]:
            to_sibling(u, 0, outs[a].at[me.yh, :, me.c, :, columns(u)])

    def forward_phase(u):
        a = units[u][0]
        y_one[u].wait_recv()
        ref = outs[a].at[1 - me.yh, :, me.c, :, columns(u, me.half)]
        y_two[u] = send(ref, ref, y_send.at[u, 1], y_recv.at[u, 1], me.inner())

    def last_phase(u):
        a = units[u][0]
        y_two[u].wait_recv()
        if units[u][3]:
            ref = outs[a].at[:, :, me.c, :, columns(u)]
            x_sent[u] = [send(ref, ref, x_send.at[u, i], x_recv.at[u, i], to) for i, to in enumerate(me.peers("x"))]
            to_sibling(u, 3, ref)
        else:
            to_sibling(u, 1, outs[a].at[1 - me.yh, :, me.c, :, columns(u)])

    def x_phase(u, i):
        x_sent[u][i].wait_recv()
        to_sibling(u, i, outs[units[u][0]].at[:, :, me.c, :, columns(u, None, (me.x + 3 - i) % 4)])

    def arrived(*which):
        for u in which:
            for at in range(4):
                if (u, at) in s_sent:
                    s_sent.pop((u, at)).wait_recv()

    cos, sin = cos_ref[...], sin_ref[...]

    def begin():
        for copy in rows:
            copy.wait()
        for copy in halo:
            copy.wait_recv()
        keep = mine_ref[...] > 0
        x_ref[...] = jnp.where(keep, x_ref[...], jnp.zeros_like(x_ref))
        dy_ref[...] = jnp.where(keep, dy_ref[...], jnp.zeros_like(dy_ref))
        arrived(0)
        for s in range(SHARDS):
            row = gains_ref[s // 8, (s // 2) % 4, s % 2, 0:1, :].astype(jnp.float32)
            gain1_ref[:, 96 * s : 96 * (s + 1)] = row[:, :96]
            gain2_ref[:, 96 * s : 96 * (s + 1)] = row[:, 128:224]
        x = x_ref[...].astype(jnp.float32)
        a1_ref[...] = (x * lax.rsqrt(mean_of(x * x) + eps_norm) * gain1_ref[...]).astype(jnp.bfloat16)
        for ref in (q_ref, k_ref, v_ref, do_ref):
            ref[:, :, HEAD_WIDTH:] = jnp.zeros((ref.shape[0], ROWS, 128 - HEAD_WIDTH), jnp.bfloat16)

    def project(weight, dst, chunk, turned):
        value = nn(a1_ref[...], weight[:, :, :, :, CHUNK * chunk : CHUNK * (chunk + 1)].reshape(D, CHUNK))
        if turned:
            value = value * cos + swap_halves(value) * sin
        split_heads(dst, chunk, value)

    def attend(first):
        allowed = allowed_pairs(seg_ref, segt_ref)
        for head in range(first, first + 4):
            p = probabilities(q_ref[head], k_ref[head // 2], allowed)
            o = nn(p.astype(jnp.bfloat16), v_ref[head // 2])
            o_ref[:, HEAD_WIDTH * head : HEAD_WIDTH * (head + 1)] = o[:, :HEAD_WIDTH].astype(jnp.bfloat16)

    def out_project(part):
        at = slice(768 * part, 768 * (part + 1))
        x2_ref[:, at] = x_ref[:, at].astype(jnp.float32) + nn(o_ref[...], wo[:, :, :, :, at].reshape(QW, 768))

    stores = []

    def give(*refs_done):
        for ref in refs_done:
            i = [k for k, one in enumerate(rows_out) if one is ref][0]
            stores.append(pltpu.make_async_copy(ref, results[i], result_sem.at[i]))
            stores[-1].start()

    yb_ref = turn_ref.at[:, :D]

    def between():
        give(a1_ref, o_ref, dy_ref)
        second_norm(x2_ref, gain2_ref, a2_ref)
        yb_ref[...] = x2_ref[...]
        da2_ref[...] = jnp.zeros_like(da2_ref)

    loads = []

    def block_load(first):
        slot = len(loads) % 2
        pair = first // FF_BLOCK
        copies = [
            pltpu.make_async_copy(wg_hbm.at[:, :, :, :, cut(first, FF_BLOCK)], wg.at[slot], block_sem.at[slot, 0]),
            pltpu.make_async_copy(wu_hbm.at[:, :, :, :, cut(first, FF_BLOCK)], wu.at[slot], block_sem.at[slot, 1]),
            pltpu.make_async_copy(wd_hbm.at[pair // 4, pair % 4], wd.at[slot], block_sem.at[slot, 2]),
        ]
        for copy in copies:
            copy.start()
        loads.append((first, slot, copies))

    done = []

    def block_compute():
        first, slot, copies = loads[len(done)]
        done.append(first)
        for copy in copies:
            copy.wait()
        feedforward_block(
            first, a2_ref, dy_ref, wg[slot].reshape(D, FF_BLOCK), wu[slot].reshape(D, FF_BLOCK), wd[slot].reshape(FF_BLOCK, D),
            hid_ref, dg_ref, du_ref, yb_ref, da2_ref,
        )

    halo = []
    for i, (src, dst) in enumerate(((tokens, x_ref), (cotangent, dy_ref))):
        for m in range(MB):
            there = dst.at[pl.ds(m * WIN + BIN, HALO)]
            halo.append(send(src.at[m, pl.ds(0, HALO)], there, h_send.at[i, m], h_recv.at[i, m], me.step(-1)))

    def quarter(i):
        return ((me.x + 3 - i) % 4) * FF_BLOCK

    def x_quarters(u):
        for i in range(3):
            x_phase(u, i)

    pieces = {
        3: [begin],
        4: [lambda: arrived(1), lambda: project(wk, k_ref, 0, True), lambda: project(wk, k_ref, 1, True)],
        5: [lambda: arrived(2), lambda: project(wv, v_ref, 0, False), lambda: project(wv, v_ref, 1, False)],
        7: [lambda: arrived(4), lambda: project(wq, q_ref, 0, True)],
        8: [lambda: project(wq, q_ref, 1, True), lambda: arrived(5)],
        9: [lambda: project(wq, q_ref, 2, True)],
        10: [lambda: project(wq, q_ref, 3, True)],
        11: [lambda: attend(0), lambda: x_quarters(GATE_ONE)],
        12: [lambda: attend(4)],
        13: [lambda: attend(8)],
        14: [lambda: attend(12)],
        15: [lambda: x_quarters(GATE_TWO), lambda: arrived(7, 8), lambda: out_project(0)],
        16: [lambda: out_project(1)],
        17: [between],
        18: [lambda: arrived(GATE_ONE, UP_X, *range(10, 16)), lambda: block_load(me.x * FF_BLOCK)],
        19: [lambda: arrived(GATE_TWO, 16), lambda: block_load(2048), block_compute],
        20: [lambda: arrived(17), lambda: x_quarters(UP_X), lambda: block_load(2048 + FF_BLOCK) , block_compute],
        21: [block_compute, lambda: arrived(18), lambda: block_load(2048 + 2 * FF_BLOCK)],
    }
    for u in range(AHEAD):
        z_phase(u)
    for t in range(count + 2):
        if t + AHEAD < count:
            z_phase(t + AHEAD)
        if t < count:
            y_phase(t)
        if 1 <= t <= count:
            forward_phase(t - 1)
        if t >= 2:
            last_phase(t - 2)
        for piece in pieces.get(t, ()):
            piece()
    arrived(UP_X)
    for i in range(3):
        block_load(quarter(i))
        block_compute()
    arrived(UP_LAST)
    block_load(2048 + 3 * FF_BLOCK)
    block_compute()
    block_compute()
    block_ref[...] = yb_ref[...].astype(jnp.bfloat16)
    give(block_ref, a2_ref, hid_ref, dg_ref, du_ref)
    dgain_ref[...] = jnp.zeros_like(dgain_ref)
    feedforward_back(dy_ref, x2_ref, da2_ref, gain2_ref, dat_ref, dgain_ref)
    give(dat_ref)
    attention_backward(
        x_ref, gain1_ref, cos_ref, sin_ref, seg_ref, segt_ref, wq, wk, wv, wo, q_ref, k_ref, v_ref, dat_ref, da2_ref, do_ref, turn_ref, dqf_ref, dkv_ref, dx_ref, dgain_ref
    )
    give(dqf_ref, dkv_ref, dx_ref, dgain_ref)
    assert not s_sent and len(done) == FF_BLOCKS and len(stores) == len(rows_out)
    for copy in stores:
        copy.wait()
    send.drain()


def layer_pass(parts, tokens, cotangent, seg, position, mine):
    low, full = jnp.bfloat16, jnp.float32
    half = HEAD_WIDTH // 2
    freq = jnp.exp(jnp.arange(half, dtype=full) * (-2.0 * math.log(rope_base) / HEAD_WIDTH))
    angle = position.astype(full)[:, None] * freq[None, :]
    cos, sin = jnp.cos(angle), jnp.sin(angle)
    cos = jnp.tile(cos, (1, 8))
    sin = jnp.tile(jnp.concatenate([-sin, sin], axis=1), (1, 4))
    count = len(GATHER_UNITS)
    outs = [jax.ShapeDtypeStruct((2, 4, 2, *parts[a].shape), low) for a in (4, 5, 6)]
    wide = [(D, low), (D, low), (D, low), (QW, low), (D, low), (FF, low), (QW, low), (2 * KVW, low), (D, low), (FF, low), (FF, low)]
    outs += [jax.ShapeDtypeStruct((ROWS, n), t) for n, t in wide] + [jax.ShapeDtypeStruct((8, D), full)]
    outs += [jax.ShapeDtypeStruct((ROWS, D), low)]
    vmem = pl.BlockSpec(memory_space=pltpu.VMEM)
    scratch = [pltpu.VMEM((2, 4, 2, *parts[a].shape), low) for a in (0, 1, 2, 3, 7)]
    scratch += [pltpu.VMEM((ROWS, D), low), pltpu.VMEM((1, D), full), pltpu.VMEM((1, D), full)]
    scratch += [pltpu.VMEM((2, 2, 4, 2, 96, FF_BLOCK), low)] * 2 + [pltpu.VMEM((2, 2, 256, D), low)]
    scratch += [pltpu.VMEM((n, ROWS, 128), low) for n in (QUERY_HEADS, KEY_VALUE_HEADS, KEY_VALUE_HEADS, QUERY_HEADS)]
    scratch += [pltpu.VMEM((ROWS, D), full), pltpu.VMEM((ROWS, D), full), pltpu.VMEM((ROWS, QW + KVW), full)]
    scratch += [pltpu.VMEM(out.shape, out.dtype) for out in outs[3:]]
    scratch += [DMA((count, 3))] * 2 + [DMA((count, 2))] * 2 + [DMA((count, 4))] * 2 + [DMA((count, 3))] * 2
    scratch += [DMA((2, MB))] * 2 + [DMA((count, 2)), DMA((2, MB)), DMA((2, 3)), DMA((13,))]
    scratch += [pltpu.VMEM((parts[a].shape[0], n), low) for a, _, n, _ in GATHER_UNITS]
    results = pl.pallas_call(
        layer_kernel,
        out_shape=outs,
        in_specs=[ANY] * 10 + [vmem] * 5,
        out_specs=[ANY] * 16,
        scratch_shapes=scratch,
        compiler_params=pltpu.CompilerParams(collective_id=1, has_side_effects=True, vmem_limit_bytes=60 * 2**20),
        name="layer",
    )(*parts, tokens, cotangent, cos, sin, seg.reshape(ROWS, 1), seg.reshape(1, ROWS), mine.astype(jnp.int32).reshape(ROWS, 1))
    return results[3:]


def body(
    tokens,
    query_weight,
    key_weight,
    value_weight,
    out_weight,
    gate_weight,
    up_weight,
    down_weight,
    attention_gain,
    feedforward_gain,
    lengths,
    deal,
    block_cotangent,
):
    me = lax.axis_index("shard")
    core = me % 2
    gains = jnp.pad(jnp.stack([attention_gain, feedforward_gain]), ((0, 0), (0, 32))).reshape(1, 256)
    gains = jnp.pad(gains, ((0, 15), (0, 0)))
    parts = (
        query_weight,
        key_weight,
        value_weight,
        out_weight,
        gate_weight,
        up_weight,
        down_weight,
        gains,
    )
    layout = [window_layout(lengths[m, 0], me * BIN) for m in range(MB)]
    seg = jnp.concatenate([one[0] + m * 64 for m, one in enumerate(layout)])
    position = jnp.concatenate([one[1] for one in layout])
    mine = jnp.concatenate([one[2] for one in layout])
    position = jnp.where(mine, position, 0)
    block_rows, input_rows, a1, o, a2, hid, dqf, dkv, dat, dg, du, dgain, dy = layer_pass(
        parts, tokens, block_cotangent, seg, position, mine
    )

    totals, gain_totals, from_before = reduce_grads(
        (a1, o, a2, hid),
        (dqf, dkv, dat, dg, du, dy),
        dgain,
        block_rows.reshape(MB, WIN, D),
        input_rows.reshape(MB, WIN, D),
    )

    results = jnp.stack([block_rows, input_rows]).reshape(2, MB, WIN, D)[:, :, :BIN]
    from_before = jnp.pad(from_before, ((0, 0), (0, 0), (0, BIN - HALO), (0, 0)))
    mine_own = jnp.stack([one[2][:BIN] for one in layout])[None, :, :, None]
    inside = jnp.stack([one[3][:BIN] for one in layout])[None, :, :, None]
    rows_out = jnp.where(mine_own, results, jnp.where(inside, from_before, 0))
    g_query, g_kv, g_out, g_gate, g_up, g_down = [total.astype(jnp.float32) for total in totals]
    gain_out = lax.dynamic_slice_in_dim(gain_totals[:2].astype(jnp.float32), core * 96, 96, axis=1)
    return (
        rows_out[0],
        rows_out[1],
        g_query,
        g_kv[:, :KVW],
        g_kv[:, KVW:],
        g_out,
        g_gate,
        g_up,
        g_down,
        gain_out[0],
        gain_out[1],
    )


def solution(mesh):
    placed = (
        P(None, ("rep", "shard"), None),
        *([P("shard", None)] * 7),
        P("shard"),
        P("shard"),
        P(None, "rep", None),
        P(None, "rep", None),
        P(None, ("rep", "shard"), None),
    )
    return jax.shard_map(
        body,
        mesh=mesh,
        in_specs=placed,
        out_specs=(
            P(None, ("rep", "shard"), None),
            P(None, ("rep", "shard"), None),
            *([P("shard", None)] * 7),
            P("shard"),
            P("shard"),
        ),
        check_vma=False,
    )
```
